256 devices in a mesh: row: 32 (over x, z), col: 8 (over y, core).
Axes of the slice: x: 4, y: 4, z: 8, core: 2. Of those that a mesh axis runs over, the one named last changes fastest.
Arguments:
- features: bfloat16 [64, 32768], P(None, ('col', 'row')), may hold values from -4 to 4
- targets: float32 [128, 32768], P(None, ('col', 'row')), may hold values from -6 to 6
Outputs:
- coefficients: float32 [128, 32768], P(None, ('col', 'row'))
- residual: float32 [128, 32768], P(None, ('col', 'row'))
- direction: float32 [128, 32768], P(None, ('col', 'row'))
The draws below stay inside these ranges and needn't reach their ends.
All inputs are finite; a program needn't handle non-finite values.
Results may differ from the reference program's by a relative error of at most 0.0061.
Values may be sent and summed in bfloat16 or wider, within the bound.
A program may use at most 64 MiB of HBM per device.

```python
import jax
import jax.numpy as jnp
from jax import lax

F = 64
R = 128
NS = 32768


def draw_features(key, part):
    values = jnp.clip(jax.random.normal(key, (F, NS), jnp.float32), -4.0, 4.0)
    return values.astype(jnp.bfloat16)


def level_of(own_key, extent, shards, least, largest):
    gain, own = 1.0, jax.random.fold_in(own_key, 6)
    for dim, shards_of in shards:
        draws = jnp.exp(jax.random.uniform(jax.random.fold_in(own, dim), (shards_of,), jnp.float32, least / len(shards), largest / len(shards)))
        gain = gain * jnp.repeat(draws, extent[dim] // shards_of).reshape([-1 if axis == dim else 1 for axis in range(len(extent))])
    return gain


def scatter_about(own_key, shape, deviation, most, pieces=(), kind=jnp.bfloat16):
    array = deviation * jax.random.normal(own_key, shape, jnp.float32)
    if pieces:
        array = array * level_of(own_key, shape, pieces, -0.22, 0.18)
    return jnp.clip(array, -most, most).astype(kind)


def setup_inputs(seed: int = 0) -> dict:
    streams_of = jax.random.split(jax.random.key(seed), 3)
    features = draw_features(jax.random.fold_in(streams_of[2], 71), 0)
    targets = scatter_about(streams_of[1], (R, NS), 1.0, 6.0, ((1, 256),), jnp.float32)
    return {"features": features, "targets": targets}


ridge_weight = 0.5
kernel_gain = 2.0
sharpness = 3.0

def kernel_rows(row_feat, row_sq, points, squares_all, panel_wide):
    inner = jnp.dot(row_feat.T, points, precision=lax.Precision.HIGHEST)
    distance = row_sq[:, None] + squares_all[None, :] - 2.0 * inner
    entries = jnp.exp(-sharpness * distance / F).astype(jnp.bfloat16)
    entries = lax.optimization_barrier(entries).astype(jnp.float32)
    return jnp.dot(panel_wide, entries.T, precision=lax.Precision.HIGHEST)

def gram(left, right):
    return lax.dot_general(left, right, (((1,), (1,)), ((), ())), precision=lax.Precision.HIGHEST)

def cholesky_factor(matrix):
    size = matrix.shape[0]
    index = jnp.arange(size, dtype=jnp.int32)

    def step(position, state):
        rest, factor = state
        pos = jnp.asarray(position).astype(jnp.int32)
        column = lax.dynamic_slice_in_dim(rest, pos, 1, 1)[:, 0]
        pivot = jnp.sqrt(lax.dynamic_slice_in_dim(column, pos, 1, 0)[0])
        column = jnp.where(index >= pos, column / pivot, jnp.zeros_like(column))
        rest = rest - column[:, None] * column[None, :]
        factor = lax.dynamic_update_slice_in_dim(factor, column[:, None], pos, 1)
        return (rest, factor)
    return lax.fori_loop(0, size, step, (matrix, jnp.zeros_like(matrix)))[1]

def solve_with(factor, rhs):
    size = factor.shape[0]

    def forward(position, solved):
        pos = jnp.asarray(position).astype(jnp.int32)
        line = lax.dynamic_slice_in_dim(factor, pos, 1, 0)
        pivot = lax.dynamic_slice_in_dim(line[0], pos, 1, 0)[0]
        value = (lax.dynamic_slice_in_dim(rhs, pos, 1, 0) - jnp.dot(line, solved, precision=lax.Precision.HIGHEST)) / pivot
        return lax.dynamic_update_slice_in_dim(solved, value, pos, 0)
    middle = lax.fori_loop(0, size, forward, jnp.zeros_like(rhs))

    def backward(step_count, solved):
        pos = (size - 1 - jnp.asarray(step_count)).astype(jnp.int32)
        line = lax.dynamic_slice_in_dim(factor, pos, 1, 1)
        pivot = lax.dynamic_slice_in_dim(line[:, 0], pos, 1, 0)[0]
        value = (lax.dynamic_slice_in_dim(middle, pos, 1, 0) - jnp.dot(line.T, solved, precision=lax.Precision.HIGHEST)) / pivot
        return lax.dynamic_update_slice_in_dim(solved, value, pos, 0)
    return lax.fori_loop(0, size, backward, jnp.zeros_like(rhs))

def reference(features, targets):
    points = features.astype(jnp.float32)
    squares_all = lax.optimization_barrier(jnp.sum(points * points, axis=0))
    panel = lax.optimization_barrier(targets.astype(jnp.bfloat16))
    panel_wide = panel.astype(jnp.float32)
    block_size = min(512, NS)
    blocks = NS // block_size
    row_blocks = points.reshape(F, blocks, block_size).transpose(1, 0, 2)
    sq_blocks = squares_all.reshape(blocks, block_size)

    def block_image(operands):
        return kernel_rows(operands[0], operands[1], points, squares_all, panel_wide)
    stacked = lax.map(block_image, (row_blocks, sq_blocks))
    kernel_image = stacked.transpose(1, 0, 2).reshape(R, NS)
    image = ridge_weight * targets + kernel_gain * kernel_image
    squares = gram(targets, targets)
    curvature = gram(targets, image)
    sym = 0.5 * (curvature + curvature.T)
    factor = cholesky_factor(sym)
    step_size = solve_with(factor, squares)
    coefficients = jnp.dot(step_size.T, targets, precision=lax.Precision.HIGHEST)
    residual = targets - jnp.dot(step_size.T, image, precision=lax.Precision.HIGHEST)
    conjugacy = gram(image, residual)
    correction = -solve_with(factor, conjugacy)
    direction = residual + jnp.dot(correction.T, targets, precision=lax.Precision.HIGHEST)
    return (coefficients, residual, direction)
```

```python
import math

import jax
import jax.numpy as jnp
from jax import lax
from jax.experimental import pallas as pl
from jax.experimental.pallas import tpu as pltpu
from jax.sharding import PartitionSpec as P

F = 64
R = 128
B = 128
X, Y, Z, C = 4, 4, 8, 2
PLANE = X * Y
LINE = Z * C

ridge_weight = 0.5
kernel_gain = 2.0
sharpness = 3.0
exponent_scale = sharpness / F * math.log2(math.e)

f32 = jnp.float32
bf16 = jnp.bfloat16


def dot_exact(left, right):
    return jnp.dot(left, right, precision=lax.Precision.HIGHEST, preferred_element_type=f32)


def norm_rows(feat, rows):
    wide = feat.astype(f32)
    total = jnp.sum(wide * wide, axis=0, keepdims=True)
    high = total.astype(bf16).astype(f32)
    mid = (total - high).astype(bf16).astype(f32)
    low = (total - high - mid).astype(bf16).astype(f32)
    width = feat.shape[1]
    index = lax.broadcasted_iota(jnp.int32, (F, width), 0)
    first = 0 if rows else 3
    other = 3 if rows else 0
    sign = 1.0 if rows else -1.0
    extra = jnp.where(index == first, sign * high, 0.0)
    extra = jnp.where(index == first + 1, sign * mid, extra)
    extra = jnp.where(index == first + 2, sign * low, extra)
    extra = jnp.where((index >= other) & (index < other + 3), sign, extra)
    scaled = wide if rows else 2.0 * wide
    return jnp.concatenate([scaled, extra], axis=0)


def sweep_inverse(matrix):
    lanes = lax.broadcasted_iota(jnp.int32, (8, R), 1)
    subs = lax.broadcasted_iota(jnp.int32, (8, R), 0)
    tiles = tuple(matrix[8 * t : 8 * t + 8, :] for t in range(R // 8))

    def eight(_, tiles):
        tiles = list(tiles)
        for p in range(8):
            head = tiles[0]
            line = jnp.broadcast_to(head[p : p + 1, :], (8, R))
            inverse = 1.0 / jnp.broadcast_to(line[:, p : p + 1], (8, R))
            at = lanes == p
            scaled = jnp.where(at, -inverse, line * inverse)
            for t in range(R // 8):
                column = jnp.broadcast_to(tiles[t][:, p : p + 1], (8, R))
                tiles[t] = jnp.where(at, 0.0, tiles[t]) - column * scaled
            tiles[0] = jnp.where(subs == p, scaled, tiles[0])
        tiles = tiles[1:] + tiles[:1]
        return tuple(pltpu.roll(tile, R - 8, 1) for tile in tiles)

    tiles = lax.fori_loop(0, R // 8, eight, tiles)
    return jnp.concatenate(tiles, axis=0)


def kernel(
    feat_ref, targ_ref, coef_ref, resid_ref, dir_ref,
    block, row_feat, row_aug, col_aug, total, outgoing, incoming,
    sq_local, sq_in, sq_sum, sq_line, sq_full,
    gr_local, gr_in, gr_sum, gr_line, gr_full,
    block_recv, block_send, row_sems, image_sems, sq_sems, gr_sems,
):
    row, col = lax.axis_index("row"), lax.axis_index("col")
    x, z = row // Z, row % Z
    y, core = col // C, col % C
    here = x * Y + y

    def at_plane(step):
        tx, ty = (x + step // Y) % X, (y + step % Y) % Y
        return (tx * Z + z, ty * C + core), tx * Y + ty

    def at_plane_back(step):
        tx, ty = (x + X - step // Y) % X, (y + Y - step % Y) % Y
        return (tx * Z + z, ty * C + core)

    def at_line(step):
        tz, tc = (z + step // C) % Z, (core + step % C) % C
        return (x * Z + tz, y * C + tc)

    sibling = (row, y * C + 1 - core)
    above = (x * Z + (z + 1) % Z, col)
    below = (x * Z + (z + Z - 1) % Z, col)

    def send(src, dst, send_sem, recv_sem, device):
        pltpu.make_async_remote_copy(
            src_ref=src, dst_ref=dst, send_sem=send_sem, recv_sem=recv_sem,
            device_id=device, device_id_type=pl.DeviceIdType.MESH,
        ).start()

    def take(ref, sem):
        pltpu.make_async_copy(ref, ref, sem).wait()

    barrier = pltpu.get_barrier_semaphore()

    def greet(step, carry):
        pl.semaphore_signal(barrier, inc=1, device_id=at_plane(step)[0], device_id_type=pl.DeviceIdType.MESH)
        pl.semaphore_signal(barrier, inc=1, device_id=at_line(step), device_id_type=pl.DeviceIdType.MESH)
        return carry

    lax.fori_loop(1, PLANE, greet, 0)

    targ = targ_ref[...]
    targ_t = targ.T
    block[0, 0:F, :] = feat_ref[...]
    block[0, F : F + R, :] = targ_t.astype(bf16)
    pl.semaphore_wait(barrier, PLANE + LINE - 2)

    def forward(slot, step, device, to):
        send(block.at[slot], block.at[to], block_send.at[step], block_recv.at[to], device)

    forward(0, 0, above, 1)
    forward(0, 1, below, 5)
    forward(0, 2, sibling, 8)

    def send_feat(step, carry):
        send(block.at[0, pl.ds(0, F)], row_feat.at[step - 1], row_sems.at[0], row_sems.at[1], at_plane(step)[0])
        return carry

    lax.fori_loop(1, PLANE, send_feat, 0)

    def reduce_plane(local, arrive, sems):
        def one(step, carry):
            device, piece = at_plane(step)
            send(local.at[piece], arrive.at[step - 1], sems.at[0], sems.at[1], device)
            return carry

        lax.fori_loop(1, PLANE, one, 0)

    def sum_line(local, arrive, own, line, sems):
        take(arrive, sems.at[1])
        own[...] = local[here] + jnp.sum(arrive[...], axis=0)

        def one(step, carry):
            send(own, line.at[step - 1], sems.at[2], sems.at[3], at_line(step))
            return carry

        lax.fori_loop(1, LINE, one, 0)

    def spread_plane(own, line, full, sems):
        take(line, sems.at[3])
        full[here] = own[...] + jnp.sum(line[...], axis=0)

        def one(step, carry):
            send(full.at[here], full.at[here], sems.at[4], sems.at[5], at_plane(step)[0])
            return carry

        lax.fori_loop(1, PLANE, one, 0)

    def finish(arrive, sems):
        take(arrive, sems.at[5])

    def settle(arrive, line, sems):
        take(arrive, sems.at[0])
        take(line, sems.at[2])
        take(arrive, sems.at[4])

    squares = dot_exact(targ, targ_t)
    sq_local[...] = squares.reshape(PLANE, 8, R)
    reduce_plane(sq_local, sq_in, sq_sems)

    row_aug[0:B, :] = norm_rows(block[0, 0:F, :], True).T.astype(bf16)
    take(row_feat, row_sems.at[1])

    def augment(slot, carry):
        row_aug[pl.ds(pl.multiple_of(slot * B, B), B), :] = norm_rows(row_feat[slot - 1], True).T.astype(bf16)
        return carry

    lax.fori_loop(1, PLANE, augment, 0)

    def columns(pair):
        feats = jnp.concatenate([block[pair, 0:F, :], block[pair + 8, 0:F, :]], axis=1)
        col_aug[pair] = norm_rows(feats, False).astype(bf16)

    def product(rows, pair):
        minus = jnp.dot(rows, col_aug[pair], preferred_element_type=f32)
        entries = jnp.exp2(minus * exponent_scale).astype(bf16)
        panel = jnp.concatenate([block[pair, F : F + R, :], block[pair + 8, F : F + R, :]], axis=0)
        return jnp.dot(entries, panel, preferred_element_type=f32)

    def gathered(pairs, first):
        for pair in pairs:
            columns(pair)

        def one(slot, carry):
            where = pl.ds(pl.multiple_of(slot * B, B), B)
            rows = row_aug[where, :]
            value = None if first else total[where, :]
            for pair in pairs:
                term = product(rows, pair)
                value = term if value is None else value + term
            total[where, :] = value
            return carry

        lax.fori_loop(0, PLANE, one, 0)

    def arrived(slot):
        take(block.at[slot], block_recv.at[slot])

    arrived(1)
    forward(1, 3, above, 2)
    forward(1, 4, sibling, 9)
    arrived(5)
    forward(5, 5, below, 6)
    forward(5, 6, sibling, 13)
    arrived(8)
    gathered((0,), True)
    arrived(2)
    forward(2, 7, above, 3)
    forward(2, 8, sibling, 10)
    arrived(6)
    forward(6, 9, below, 7)
    forward(6, 10, sibling, 14)
    sum_line(sq_local, sq_in, sq_sum, sq_line, sq_sems)
    arrived(9)
    arrived(13)
    gathered((1, 5), False)
    arrived(3)
    forward(3, 11, above, 4)
    forward(3, 12, sibling, 11)
    arrived(7)
    forward(7, 13, sibling, 15)
    spread_plane(sq_sum, sq_line, sq_full, sq_sems)
    arrived(10)
    arrived(14)
    gathered((2, 6), False)
    arrived(4)
    forward(4, 14, sibling, 12)
    arrived(11)
    arrived(15)
    arrived(12)
    last = (3, 7, 4)
    for pair in last:
        columns(pair)

    def part(slot):
        where = pl.ds(pl.multiple_of(slot * B, B), B)
        rows = row_aug[where, :]
        value = total[where, :]
        for pair in last:
            value = value + product(rows, pair)
        return value

    def finish_rows(slot, carry):
        outgoing[slot - 1] = part(slot).astype(bf16)
        send(outgoing.at[slot - 1], incoming.at[slot - 1], image_sems.at[0], image_sems.at[1], at_plane_back(slot))
        return carry

    lax.fori_loop(1, PLANE, finish_rows, 0)
    own = part(0)
    take(incoming, image_sems.at[1])

    def add(slot, carry):
        return carry + incoming[slot].astype(f32)

    kernel_image_t = lax.fori_loop(0, PLANE - 1, add, own)
    image_t = ridge_weight * targ_t + kernel_gain * kernel_image_t
    image = image_t.T
    gr_local[:, 0:8, :] = dot_exact(targ, image_t).reshape(PLANE, 8, R)
    gr_local[:, 8:16, :] = dot_exact(image, image_t).reshape(PLANE, 8, R)
    reduce_plane(gr_local, gr_in, gr_sems)
    sum_line(gr_local, gr_in, gr_sum, gr_line, gr_sems)
    spread_plane(gr_sum, gr_line, gr_full, gr_sems)
    finish(sq_in, sq_sems)
    finish(gr_in, gr_sems)

    squares = sq_full[...].reshape(R, R)
    curvature = gr_full[:, 0:8, :].reshape(R, R)
    image_gram = gr_full[:, 8:16, :].reshape(R, R)
    curvature_t = curvature.T
    minus_inverse = sweep_inverse(0.5 * (curvature + curvature_t))
    step_size = -dot_exact(minus_inverse, squares)
    conjugacy = curvature_t - dot_exact(image_gram, step_size)
    correction = dot_exact(minus_inverse, conjugacy)
    step_t = step_size.T
    coef_ref[...] = dot_exact(step_t, targ)
    residual = targ - dot_exact(step_t, image)
    resid_ref[...] = residual
    dir_ref[...] = residual + dot_exact(correction.T, targ)

    take(row_feat, row_sems.at[0])
    take(incoming, image_sems.at[0])
    settle(sq_in, sq_line, sq_sems)
    settle(gr_in, gr_line, gr_sems)
    for step in range(15):
        take(block.at[0], block_send.at[step])


def local(features, targets):
    whole = jax.ShapeDtypeStruct((R, B), f32)
    vmem = pl.BlockSpec(memory_space=pltpu.VMEM)
    dma = pltpu.SemaphoreType.DMA
    return pl.pallas_call(
        kernel,
        out_shape=(whole, whole, whole),
        in_specs=[vmem, vmem],
        out_specs=(vmem, vmem, vmem),
        scratch_shapes=[
            pltpu.VMEM((LINE, F + R, B), bf16),
            pltpu.VMEM((PLANE - 1, F, B), bf16),
            pltpu.VMEM((PLANE * B, 2 * F), bf16),
            pltpu.VMEM((LINE // 2, 2 * F, 2 * B), bf16),
            pltpu.VMEM((PLANE * B, R), f32),
            pltpu.VMEM((PLANE - 1, B, R), bf16),
            pltpu.VMEM((PLANE - 1, B, R), bf16),
            pltpu.VMEM((PLANE, 8, R), f32),
            pltpu.VMEM((PLANE - 1, 8, R), f32),
            pltpu.VMEM((8, R), f32),
            pltpu.VMEM((LINE - 1, 8, R), f32),
            pltpu.VMEM((PLANE, 8, R), f32),
            pltpu.VMEM((PLANE, 16, R), f32),
            pltpu.VMEM((PLANE - 1, 16, R), f32),
            pltpu.VMEM((16, R), f32),
            pltpu.VMEM((LINE - 1, 16, R), f32),
            pltpu.VMEM((PLANE, 16, R), f32),
            dma((LINE,)),
            dma((15,)),
            dma((2,)),
            dma((2,)),
            dma((6,)),
            dma((6,)),
        ],
        compiler_params=pltpu.CompilerParams(
            collective_id=0, has_side_effects=True, vmem_limit_bytes=32 * 1024 * 1024
        ),
    )(features, targets)


def solution(mesh):
    spec = P(None, ("col", "row"))
    return jax.shard_map(
        local, mesh=mesh, in_specs=(spec, spec), out_specs=(spec, spec, spec), check_vma=False
    )
```

```python
import math

import jax
import jax.numpy as jnp
from jax import lax
from jax.experimental import pallas as pl
from jax.experimental.pallas import tpu as pltpu
from jax.sharding import PartitionSpec as P

F = 64
R = 128
B = 128
X, Y, Z, C = 4, 4, 8, 2
PLANE = X * Y
LINE = Z * C
EARLY = 5

ridge_weight = 0.5
kernel_gain = 2.0
sharpness = 3.0
exponent_scale = sharpness / F * math.log2(math.e)

f32 = jnp.float32
bf16 = jnp.bfloat16


def dot_exact(left, right):
    return jnp.dot(left, right, precision=lax.Precision.HIGHEST, preferred_element_type=f32)


def norm_rows(feat, rows):
    wide = feat.astype(f32)
    total = jnp.sum(wide * wide, axis=0, keepdims=True)
    high = total.astype(bf16).astype(f32)
    mid = (total - high).astype(bf16).astype(f32)
    low = (total - high - mid).astype(bf16).astype(f32)
    width = feat.shape[1]
    index = lax.broadcasted_iota(jnp.int32, (F, width), 0)
    first = 0 if rows else 3
    other = 3 if rows else 0
    sign = 1.0 if rows else -1.0
    extra = jnp.where(index == first, sign * high, 0.0)
    extra = jnp.where(index == first + 1, sign * mid, extra)
    extra = jnp.where(index == first + 2, sign * low, extra)
    extra = jnp.where((index >= other) & (index < other + 3), sign, extra)
    scaled = wide if rows else 2.0 * wide
    return jnp.concatenate([scaled, extra], axis=0)


def sweep_inverse(matrix):
    lanes = lax.broadcasted_iota(jnp.int32, (8, R), 1)
    subs = lax.broadcasted_iota(jnp.int32, (8, R), 0)
    low = lanes < 8

    def spread_lane(tile, lane):
        return jnp.broadcast_to(tile[:, lane : lane + 1], (8, R))

    def spread_line(tile, sub):
        return jnp.broadcast_to(tile[sub : sub + 1, :], (8, R))

    def eight(_, tiles):
        head = tiles[0]
        cols = [spread_lane(head, p) for p in range(8)]
        pivot = {(s, t): spread_line(cols[t], s) for t in range(8) for s in range(t + 1)}
        rows = [jnp.where(low, jnp.where(lanes == p, -1.0, 0.0), spread_line(head, p)) for p in range(8)]
        for p in range(8):
            inverse = 1.0 / pivot[p, p]
            rows[p] = rows[p] * inverse
            ahead = {t: pivot[p, t] * inverse for t in range(p + 1, 8)}
            for s in range(8):
                if s != p:
                    rows[s] = rows[s] - pivot[min(s, p), max(s, p)] * rows[p]
            for t in range(p + 1, 8):
                for s in range(t + 1):
                    if s < p:
                        pivot[s, t] = pivot[s, t] - pivot[s, p] * ahead[t]
                    elif s > p:
                        pivot[s, t] = pivot[s, t] - pivot[p, s] * ahead[t]
            for t in ahead:
                pivot[p, t] = ahead[t]
        turned = []
        for tile in tiles[1:]:
            terms = [spread_lane(tile, p) * rows[p] for p in range(8)]
            while len(terms) > 1:
                terms = [terms[k] + terms[k + 1] for k in range(0, len(terms), 2)]
            turned.append(jnp.where(low, 0.0, tile) - terms[0])
        swept = rows[7]
        for p in range(7):
            swept = jnp.where(subs == p, rows[p], swept)
        turned.append(swept)
        return tuple(pltpu.roll(tile, R - 8, 1) for tile in turned)

    tiles = tuple(matrix[8 * t : 8 * t + 8, :] for t in range(R // 8))
    return jnp.concatenate(lax.fori_loop(0, R // 8, eight, tiles), axis=0)


def kernel(
    feat_ref, targ_ref, coef_ref, resid_ref, dir_ref,
    block, row_feat, row_aug, col_aug, total, outgoing, incoming,
    sq_local, sq_in, sq_sum, sq_line, sq_full,
    gr_local, gr_in, gr_sum, gr_line, gr_full,
    block_recv, cross_send, line_send, row_sems, image_sems, sq_sems, gr_sems,
):
    row, col = lax.axis_index("row"), lax.axis_index("col")
    x, z = row // Z, row % Z
    y, core = col // C, col % C
    here = x * Y + y

    def at_plane(step):
        tx, ty = (x + step // Y) % X, (y + step % Y) % Y
        return (tx * Z + z, ty * C + core), tx * Y + ty

    def at_plane_back(step):
        tx, ty = (x + X - step // Y) % X, (y + Y - step % Y) % Y
        return (tx * Z + z, ty * C + core)

    def at_line(step):
        tz, tc = (z + step // C) % Z, (core + step % C) % C
        return (x * Z + tz, y * C + tc)

    sibling = (row, y * C + 1 - core)

    def up(step):
        return (x * Z + (z + step) % Z, col)

    def send(src, dst, send_sem, recv_sem, device):
        pltpu.make_async_remote_copy(
            src_ref=src, dst_ref=dst, send_sem=send_sem, recv_sem=recv_sem,
            device_id=device, device_id_type=pl.DeviceIdType.MESH,
        ).start()

    def take(ref, sem):
        pltpu.make_async_copy(ref, ref, sem).wait()

    barrier = pltpu.get_barrier_semaphore()

    def greet(step, carry):
        pl.semaphore_signal(barrier, inc=1, device_id=at_plane(step)[0], device_id_type=pl.DeviceIdType.MESH)
        pl.semaphore_signal(barrier, inc=1, device_id=at_line(step), device_id_type=pl.DeviceIdType.MESH)
        return carry

    lax.fori_loop(1, PLANE, greet, 0)

    targ = targ_ref[...]
    targ_t = targ.T
    block[0, 0:F, :] = feat_ref[...]
    block[0, F : F + R, :] = targ_t.astype(bf16)
    squares = dot_exact(targ, targ_t)
    sq_local[...] = squares.reshape(PLANE, 8, R)
    row_aug[0:B, :] = norm_rows(block[0, 0:F, :], True).T.astype(bf16)
    pl.semaphore_wait(barrier, PLANE + LINE - 2)

    def order(step):
        return jnp.where(step % 2 == 1, (step + 1) // 2, (Z - step // 2) % Z)

    def across(slot):
        send(block.at[slot], block.at[slot + Z], cross_send.at[slot], block_recv.at[slot + Z], sibling)

    def send_block(step, carry):
        slot = order(step)
        send(block.at[0], block.at[slot], line_send.at[0], block_recv.at[slot], up(slot))
        return carry

    def send_feat(step, carry):
        send(block.at[0, pl.ds(0, F)], row_feat.at[step - 1], row_sems.at[0], row_sems.at[1], at_plane(step)[0])
        return carry

    across(0)
    lax.fori_loop(1, PLANE, send_feat, 0)
    lax.fori_loop(1, Z, send_block, 0)

    def reduce_plane(local, arrive, sems):
        def one(step, carry):
            device, piece = at_plane(step)
            send(local.at[piece], arrive.at[step - 1], sems.at[0], sems.at[1], device)
            return carry

        lax.fori_loop(1, PLANE, one, 0)

    def sum_line(local, arrive, own, line, sems):
        take(arrive, sems.at[1])
        own[...] = local[here] + jnp.sum(arrive[...], axis=0)

        def one(step, carry):
            send(own, line.at[step - 1], sems.at[2], sems.at[3], at_line(step))
            return carry

        lax.fori_loop(1, LINE, one, 0)

    def spread_plane(own, line, full, sems):
        take(line, sems.at[3])
        full[here] = own[...] + jnp.sum(line[...], axis=0)

        def one(step, carry):
            send(full.at[here], full.at[here], sems.at[4], sems.at[5], at_plane(step)[0])
            return carry

        lax.fori_loop(1, PLANE, one, 0)

    def finish(arrive, sems):
        take(arrive, sems.at[5])

    def settle(arrive, line, sems):
        take(arrive, sems.at[0])
        take(line, sems.at[2])
        take(arrive, sems.at[4])

    reduce_plane(sq_local, sq_in, sq_sems)

    def arrived(slot):
        take(block.at[slot], block_recv.at[slot])

    def pass_on(step, carry):
        arrived(order(step))
        across(order(step))
        return carry

    lax.fori_loop(1, 3, pass_on, 0)
    take(row_feat, row_sems.at[1])

    def augment(slot, carry):
        row_aug[pl.ds(pl.multiple_of(slot * B, B), B), :] = norm_rows(row_feat[slot - 1], True).T.astype(bf16)
        return carry

    lax.fori_loop(1, PLANE, augment, 0)

    def columns(pair):
        arrived(pair + Z)
        feats = jnp.concatenate([block[pair, 0:F, :], block[pair + Z, 0:F, :]], axis=1)
        col_aug[pair] = norm_rows(feats, False).astype(bf16)

    def product(rows, pair):
        minus = jnp.dot(rows, col_aug[pair], preferred_element_type=f32)
        entries = jnp.exp2(minus * exponent_scale).astype(bf16)
        panel = jnp.concatenate([block[pair, F : F + R, :], block[pair + Z, F : F + R, :]], axis=0)
        return jnp.dot(entries, panel, preferred_element_type=f32)

    def gathered(step, carry):
        pair = order(step)
        columns(pair)
        total[...] += product(row_aug[...], pair)
        return carry

    columns(0)
    total[...] = product(row_aug[...], 0)
    lax.fori_loop(3, EARLY, pass_on, 0)
    lax.fori_loop(1, 3, gathered, 0)
    lax.fori_loop(EARLY, Z, pass_on, 0)
    lax.fori_loop(3, EARLY, gathered, 0)
    sum_line(sq_local, sq_in, sq_sum, sq_line, sq_sems)
    last = [(step + 1) // 2 if step % 2 else Z - step // 2 for step in range(EARLY, Z)]
    for pair in last:
        columns(pair)

    def part(dx):
        where = pl.ds(pl.multiple_of(dx * Y * B, Y * B), Y * B)
        rows = row_aug[where, :]
        value = total[where, :]
        for pair in last:
            value = value + product(rows, pair)
        return value

    def send_rows(slot):
        send(outgoing.at[slot], incoming.at[slot], image_sems.at[0], image_sems.at[1], at_plane_back(slot))

    def finish_rows(step, carry):
        dx = 2 + step - 3 * (step // 2)
        outgoing[pl.ds(dx * Y, Y)] = part(dx).astype(bf16).reshape(Y, B, R)
        for dy in (2, 1, 3, 0):
            send_rows(dx * Y + dy)
        return carry

    lax.fori_loop(0, X - 1, finish_rows, 0)
    own = part(0)
    outgoing[pl.ds(0, Y)] = own.astype(bf16).reshape(Y, B, R)
    for dy in (2, 1, 3):
        send_rows(dy)
    own = own[0:B, :]
    spread_plane(sq_sum, sq_line, sq_full, sq_sems)
    others = incoming.at[pl.ds(1, PLANE - 1)]
    take(others, image_sems.at[1])

    def add(slot, carry):
        return carry + incoming[slot].astype(f32)

    kernel_image_t = lax.fori_loop(1, PLANE, add, own)
    image_t = ridge_weight * targ_t + kernel_gain * kernel_image_t
    image = image_t.T
    gr_local[:, 0:8, :] = dot_exact(targ, image_t).reshape(PLANE, 8, R)
    gr_local[:, 8:16, :] = dot_exact(image, image_t).reshape(PLANE, 8, R)
    reduce_plane(gr_local, gr_in, gr_sems)
    sum_line(gr_local, gr_in, gr_sum, gr_line, gr_sems)
    spread_plane(gr_sum, gr_line, gr_full, gr_sems)
    finish(sq_in, sq_sems)
    finish(gr_in, gr_sems)

    squares = sq_full[...].reshape(R, R)
    curvature = gr_full[:, 0:8, :].reshape(R, R)
    image_gram = gr_full[:, 8:16, :].reshape(R, R)
    curvature_t = curvature.T
    minus_inverse = sweep_inverse(0.5 * (curvature + curvature_t))
    step_size = -dot_exact(minus_inverse, squares)
    conjugacy = curvature_t - dot_exact(image_gram, step_size)
    correction = dot_exact(minus_inverse, conjugacy)
    step_t = step_size.T
    coef_ref[...] = dot_exact(step_t, targ)
    residual = targ - dot_exact(step_t, image)
    resid_ref[...] = residual
    dir_ref[...] = residual + dot_exact(correction.T, targ)

    take(row_feat, row_sems.at[0])
    take(others, image_sems.at[0])
    settle(sq_in, sq_line, sq_sems)
    settle(gr_in, gr_line, gr_sems)
    take(block.at[pl.ds(1, Z - 1)], line_send.at[0])
    for slot in range(Z):
        take(block.at[slot], cross_send.at[slot])


def local(features, targets):
    whole = jax.ShapeDtypeStruct((R, B), f32)
    vmem = pl.BlockSpec(memory_space=pltpu.VMEM)
    dma = pltpu.SemaphoreType.DMA
    return pl.pallas_call(
        kernel,
        out_shape=(whole, whole, whole),
        in_specs=[vmem, vmem],
        out_specs=(vmem, vmem, vmem),
        scratch_shapes=[
            pltpu.VMEM((LINE, F + R, B), bf16),
            pltpu.VMEM((PLANE - 1, F, B), bf16),
            pltpu.VMEM((PLANE * B, 2 * F), bf16),
            pltpu.VMEM((LINE // 2, 2 * F, 2 * B), bf16),
            pltpu.VMEM((PLANE * B, R), f32),
            pltpu.VMEM((PLANE, B, R), bf16),
            pltpu.VMEM((PLANE, B, R), bf16),
            pltpu.VMEM((PLANE, 8, R), f32),
            pltpu.VMEM((PLANE - 1, 8, R), f32),
            pltpu.VMEM((8, R), f32),
            pltpu.VMEM((LINE - 1, 8, R), f32),
            pltpu.VMEM((PLANE, 8, R), f32),
            pltpu.VMEM((PLANE, 16, R), f32),
            pltpu.VMEM((PLANE - 1, 16, R), f32),
            pltpu.VMEM((16, R), f32),
            pltpu.VMEM((LINE - 1, 16, R), f32),
            pltpu.VMEM((PLANE, 16, R), f32),
            dma((LINE,)),
            dma((Z,)),
            dma((1,)),
            dma((2,)),
            dma((2,)),
            dma((6,)),
            dma((6,)),
        ],
        compiler_params=pltpu.CompilerParams(
            collective_id=0, has_side_effects=True, vmem_limit_bytes=32 * 1024 * 1024
        ),
    )(features, targets)


def solution(mesh):
    spec = P(None, ("col", "row"))
    return jax.shard_map(
        local, mesh=mesh, in_specs=(spec, spec), out_specs=(spec, spec, spec), check_vma=False
    )
```

```python
import math

import jax
import jax.numpy as jnp
from jax import lax
from jax.experimental import pallas as pl
from jax.experimental.pallas import tpu as pltpu
from jax.sharding import PartitionSpec as P

F = 64
R = 128
B = 128
X, Y, Z, C = 4, 4, 8, 2
PLANE = X * Y
LINE = Z * C
EARLY = 5
VMEMLIM = 60

ridge_weight = 0.5
kernel_gain = 2.0
sharpness = 3.0
exponent_scale = sharpness / F * math.log2(math.e)

f32 = jnp.float32
bf16 = jnp.bfloat16


def dot_exact(left, right):
    return jnp.dot(left, right, precision=lax.Precision.HIGHEST, preferred_element_type=f32)


def norm_rows(feat, rows):
    wide = feat.astype(f32)
    total = jnp.sum(wide * wide, axis=0, keepdims=True)
    high = total.astype(bf16).astype(f32)
    mid = (total - high).astype(bf16).astype(f32)
    low = (total - high - mid).astype(bf16).astype(f32)
    width = feat.shape[1]
    index = lax.broadcasted_iota(jnp.int32, (F, width), 0)
    first = 0 if rows else 3
    other = 3 if rows else 0
    sign = 1.0 if rows else -1.0
    extra = jnp.where(index == first, sign * high, 0.0)
    extra = jnp.where(index == first + 1, sign * mid, extra)
    extra = jnp.where(index == first + 2, sign * low, extra)
    extra = jnp.where((index >= other) & (index < other + 3), sign, extra)
    scaled = wide if rows else 2.0 * wide
    return jnp.concatenate([scaled, extra], axis=0)


def sweep_inverse(matrix):
    lanes = lax.broadcasted_iota(jnp.int32, (8, R), 1)
    subs = lax.broadcasted_iota(jnp.int32, (8, R), 0)
    low = lanes < 8

    def spread_lane(tile, lane):
        return jnp.broadcast_to(tile[:, lane : lane + 1], (8, R))

    def spread_line(tile, sub):
        return jnp.broadcast_to(tile[sub : sub + 1, :], (8, R))

    def eight(_, tiles):
        head = tiles[0]
        cols = [spread_lane(head, p) for p in range(8)]
        pivot = {(s, t): spread_line(cols[t], s) for t in range(8) for s in range(t + 1)}
        rows = [jnp.where(low, jnp.where(lanes == p, -1.0, 0.0), spread_line(head, p)) for p in range(8)]
        for p in range(8):
            inverse = 1.0 / pivot[p, p]
            rows[p] = rows[p] * inverse
            ahead = {t: pivot[p, t] * inverse for t in range(p + 1, 8)}
            for s in range(8):
                if s != p:
                    rows[s] = rows[s] - pivot[min(s, p), max(s, p)] * rows[p]
            for t in range(p + 1, 8):
                for s in range(t + 1):
                    if s < p:
                        pivot[s, t] = pivot[s, t] - pivot[s, p] * ahead[t]
                    elif s > p:
                        pivot[s, t] = pivot[s, t] - pivot[p, s] * ahead[t]
            for t in ahead:
                pivot[p, t] = ahead[t]
        turned = []
        for tile in tiles[1:]:
            terms = [spread_lane(tile, p) * rows[p] for p in range(8)]
            while len(terms) > 1:
                terms = [terms[k] + terms[k + 1] for k in range(0, len(terms), 2)]
            turned.append(jnp.where(low, 0.0, tile) - terms[0])
        swept = rows[7]
        for p in range(7):
            swept = jnp.where(subs == p, rows[p], swept)
        turned.append(swept)
        return tuple(pltpu.roll(tile, R - 8, 1) for tile in turned)

    tiles = tuple(matrix[8 * t : 8 * t + 8, :] for t in range(R // 8))
    return jnp.concatenate(lax.fori_loop(0, R // 8, eight, tiles, unroll=4), axis=0)


def kernel(
    feat_ref, targ_ref, coef_ref, taken_ref, added_ref,
    targ_own, block, row_feat, row_targ, row_aug, col_aug, total, outgoing, incoming,
    sq_local, sq_in, sq_sum, sq_line, sq_full,
    cu_local, cu_in, cu_sum, cu_line, cu_full,
    gr_local, gr_in, gr_sum, gr_line, gr_full,
    load_sems, block_recv, cross_send, line_send, row_recv, row_send, targ_sems, image_sems, sq_sems, cu_sems, gr_sems,
):
    row, col = lax.axis_index("row"), lax.axis_index("col")
    x, z = row // Z, row % Z
    y, core = col // C, col % C
    here = x * Y + y

    def at_plane(step):
        tx, ty = (x + step // Y) % X, (y + step % Y) % Y
        return (tx * Z + z, ty * C + core), tx * Y + ty

    def at_plane_back(step):
        tx, ty = (x + X - step // Y) % X, (y + Y - step % Y) % Y
        return (tx * Z + z, ty * C + core)

    def at_line(step):
        tz, tc = (z + step // C) % Z, (core + step % C) % C
        return (x * Z + tz, y * C + tc)

    sibling = (row, y * C + 1 - core)

    def up(step):
        return (x * Z + (z + step) % Z, col)

    def send(src, dst, send_sem, recv_sem, device):
        pltpu.make_async_remote_copy(
            src_ref=src, dst_ref=dst, send_sem=send_sem, recv_sem=recv_sem,
            device_id=device, device_id_type=pl.DeviceIdType.MESH,
        ).start()

    def take(ref, sem):
        pltpu.make_async_copy(ref, ref, sem).wait()

    barrier = pltpu.get_barrier_semaphore()

    def greet(step, carry):
        pl.semaphore_signal(barrier, inc=1, device_id=at_plane(step)[0], device_id_type=pl.DeviceIdType.MESH)
        pl.semaphore_signal(barrier, inc=1, device_id=at_line(step), device_id_type=pl.DeviceIdType.MESH)
        return carry

    lax.fori_loop(1, PLANE, greet, 0)

    load_feat = pltpu.make_async_copy(feat_ref, block.at[0, pl.ds(0, F)], load_sems.at[0])
    load_targ = pltpu.make_async_copy(targ_ref, targ_own, load_sems.at[1])
    load_targ.start()
    load_feat.start()
    load_targ.wait()
    load_feat.wait()
    targ = targ_own[...]
    targ_t = targ.T
    targ_high = targ.astype(bf16)
    row_targ[0] = targ_high
    block[0, F : F + R, :] = targ_t.astype(bf16)
    pl.semaphore_wait(barrier, PLANE + LINE - 2)

    def order(step):
        return jnp.where(step % 2 == 1, (step + 1) // 2, (Z - step // 2) % Z)

    def across(slot):
        send(block.at[slot], block.at[slot + Z], cross_send.at[slot], block_recv.at[slot + Z], sibling)

    def send_block(slot):
        send(block.at[0], block.at[slot], line_send.at[0], block_recv.at[slot], up(slot))

    def plane_order(step):
        turn = step // Y
        return (turn + turn // 2 - 2 * (turn // 3)) * Y + step % Y

    def send_feat(step, carry):
        slot = plane_order(PLANE - step)
        send(block.at[0, pl.ds(0, F)], row_feat.at[slot], row_send.at[0], row_recv.at[slot], at_plane(slot)[0])
        return carry

    def send_targ(step, carry):
        send(row_targ.at[0], row_targ.at[step], targ_sems.at[0], targ_sems.at[1], at_plane(step)[0])
        return carry

    for slot in (2, Z - 2, 1, Z - 1):
        send_block(slot)
    lax.fori_loop(1, PLANE, send_feat, 0)
    across(0)

    def reduce_plane(local, arrive, sems):
        def one(step, carry):
            device, piece = at_plane(step)
            send(local.at[piece], arrive.at[step - 1], sems.at[0], sems.at[1], device)
            return carry

        lax.fori_loop(1, PLANE, one, 0)

    def sum_line(local, arrive, own, line, sems):
        take(arrive, sems.at[1])
        own[...] = local[here] + jnp.sum(arrive[...], axis=0)

        def one(step, carry):
            send(own, line.at[step - 1], sems.at[2], sems.at[3], at_line(step))
            return carry

        lax.fori_loop(1, LINE, one, 0)

    def spread_plane(own, line, full, sems):
        take(line, sems.at[3])
        full[here] = own[...] + jnp.sum(line[...], axis=0)

        def one(step, carry):
            send(full.at[here], full.at[here], sems.at[4], sems.at[5], at_plane(step)[0])
            return carry

        lax.fori_loop(1, PLANE, one, 0)

    def finish(arrive, sems):
        take(arrive, sems.at[5])

    def settle(arrive, line, sems):
        take(arrive, sems.at[0])
        take(line, sems.at[2])
        take(arrive, sems.at[4])

    sq_local[...] = dot_exact(targ, targ_t).reshape(PLANE, 8, R)
    reduce_plane(sq_local, sq_in, sq_sems)
    lax.fori_loop(1, PLANE, send_targ, 0)
    row_aug[0:B, :] = norm_rows(block[0, 0:F, :], True).T.astype(bf16)

    def arrived(slot):
        take(block.at[slot], block_recv.at[slot])

    def pass_on(step, carry):
        arrived(order(step))
        across(order(step))
        return carry


    def augment(step, carry):
        slot = plane_order(step)
        take(row_feat.at[slot], row_recv.at[slot])
        row_aug[pl.ds(pl.multiple_of(slot * B, B), B), :] = norm_rows(row_feat[slot], True).T.astype(bf16)
        return carry

    lax.fori_loop(1, PLANE // 2, augment, 0)

    half = (F + R) // 2
    for slot, direction, first in ((2, 1, 0), (Z - 2, Z - 1, half)):
        arrived(slot)
        to = (slot + direction) % Z
        send(block.at[slot], block.at[to], line_send.at[1], block_recv.at[to], up(direction))
        rows = pl.ds(first, half)
        send(block.at[slot, rows], block.at[4, rows], line_send.at[1], block_recv.at[4], up(slot))
        across(slot)
    lax.fori_loop(PLANE // 2, PLANE, augment, 0)

    def columns(pair):
        arrived(pair + Z)
        feats = jnp.concatenate([block[pair, 0:F, :], block[pair + Z, 0:F, :]], axis=1)
        col_aug[pair] = norm_rows(feats, False).astype(bf16)

    def product(rows, pair):
        minus = jnp.dot(rows, col_aug[pair], preferred_element_type=f32)
        entries = jnp.exp2(minus * exponent_scale).astype(bf16)
        panel = jnp.concatenate([block[pair, F : F + R, :], block[pair + Z, F : F + R, :]], axis=0)
        return jnp.dot(entries, panel, preferred_element_type=f32)

    def gathered(step, carry):
        pair = order(step)
        columns(pair)
        total[...] += product(row_aug[...], pair)
        return carry

    lax.fori_loop(1, 3, pass_on, 0)
    columns(0)
    total[...] = product(row_aug[...], 0)
    lax.fori_loop(1, EARLY - 1, gathered, 0)
    lax.fori_loop(EARLY, Z, pass_on, 0)
    lax.fori_loop(EARLY - 1, EARLY, gathered, 0)
    sum_line(sq_local, sq_in, sq_sum, sq_line, sq_sems)
    last = [(step + 1) // 2 if step % 2 else Z - step // 2 for step in range(EARLY, Z)]
    for pair in last:
        columns(pair)

    def part(dx):
        where = pl.ds(pl.multiple_of(dx * Y * B, Y * B), Y * B)
        rows = row_aug[where, :]
        value = total[where, :]
        for pair in last:
            value = value + product(rows, pair)
        return value

    def send_rows(slot):
        send(outgoing.at[slot], incoming.at[slot], image_sems.at[0], image_sems.at[1], at_plane_back(slot))

    def finish_rows(step, carry):
        dx = 2 + step - 3 * (step // 2)
        outgoing[pl.ds(dx * Y, Y)] = part(dx).astype(bf16).reshape(Y, B, R)
        for dy in (2, 1, 3, 0):
            send_rows(dx * Y + dy)
        return carry

    lax.fori_loop(0, X - 1, finish_rows, 0)
    own = part(0)
    outgoing[pl.ds(1, Y - 1)] = own[B:, :].astype(bf16).reshape(Y - 1, B, R)
    for dy in (2, 1, 3):
        send_rows(dy)
    own = own[0:B, :]
    row_targs = row_targ.at[pl.ds(1, PLANE - 1)]
    take(row_targs, targ_sems.at[1])
    targs = jnp.concatenate([row_targ[slot] for slot in range(1, PLANE)], axis=1)
    images = outgoing[pl.ds(1, PLANE - 1)].reshape((PLANE - 1) * B, R)
    term = dot_exact(targ, own) + jnp.dot(targs, images, preferred_element_type=f32)
    cu_local[...] = ridge_weight * sq_local[...] + kernel_gain * term.reshape(PLANE, 8, R)
    reduce_plane(cu_local, cu_in, cu_sems)

    others = incoming.at[pl.ds(1, PLANE - 1)]
    take(others, image_sems.at[1])

    def add(slot, carry):
        return carry + incoming[slot].astype(f32)

    kernel_image_t = lax.fori_loop(1, PLANE, add, own)
    image_t = ridge_weight * targ_t + kernel_gain * kernel_image_t
    image = image_t.T
    gr_local[...] = dot_exact(image, image_t).reshape(PLANE, 8, R)
    reduce_plane(gr_local, gr_in, gr_sems)
    sum_line(cu_local, cu_in, cu_sum, cu_line, cu_sems)
    spread_plane(sq_sum, sq_line, sq_full, sq_sems)
    sum_line(gr_local, gr_in, gr_sum, gr_line, gr_sems)
    spread_plane(cu_sum, cu_line, cu_full, cu_sems)
    spread_plane(gr_sum, gr_line, gr_full, gr_sems)

    finish(cu_in, cu_sems)
    curvature = cu_full[...].reshape(R, R)
    curvature_t = curvature.T
    minus_inverse = sweep_inverse(0.5 * (curvature + curvature_t))
    finish(sq_in, sq_sems)
    squares = sq_full[...].reshape(R, R)
    step_size = -dot_exact(minus_inverse, squares)
    step_t = step_size.T
    coef_ref[...] = dot_exact(step_t, targ)
    taken_ref[...] = dot_exact(step_t, image)
    solved = dot_exact(minus_inverse, targ)
    before = dot_exact(curvature, solved)
    finish(gr_in, gr_sems)
    image_gram = gr_full[...].reshape(R, R)
    added_ref[...] = before - dot_exact(step_t, dot_exact(image_gram, solved))

    take(row_feat.at[pl.ds(1, PLANE - 1)], row_send.at[0])
    take(row_targs, targ_sems.at[0])
    take(others, image_sems.at[0])
    settle(sq_in, sq_line, sq_sems)
    settle(cu_in, cu_line, cu_sems)
    settle(gr_in, gr_line, gr_sems)
    take(block.at[pl.ds(1, 4)], line_send.at[0])
    take(block.at[pl.ds(1, 3)], line_send.at[1])
    for slot in range(Z):
        take(block.at[slot], cross_send.at[slot])


def local(features, targets):
    whole = jax.ShapeDtypeStruct((R, B), f32)
    vmem = pl.BlockSpec(memory_space=pltpu.VMEM)
    hbm = pl.BlockSpec(memory_space=pltpu.HBM)
    dma = pltpu.SemaphoreType.DMA
    sums = [
        pltpu.VMEM((PLANE, 8, R), f32),
        pltpu.VMEM((PLANE - 1, 8, R), f32),
        pltpu.VMEM((8, R), f32),
        pltpu.VMEM((LINE - 1, 8, R), f32),
        pltpu.VMEM((PLANE, 8, R), f32),
    ]
    coefficients, taken, added = pl.pallas_call(
        kernel,
        out_shape=(whole, whole, whole),
        in_specs=[hbm, hbm],
        out_specs=(vmem, vmem, vmem),
        scratch_shapes=[
            pltpu.VMEM((R, B), f32),
            pltpu.VMEM((LINE, F + R, B), bf16),
            pltpu.VMEM((PLANE, F, B), bf16),
            pltpu.VMEM((PLANE, R, B), bf16),
            pltpu.VMEM((PLANE * B, 2 * F), bf16),
            pltpu.VMEM((LINE // 2, 2 * F, 2 * B), bf16),
            pltpu.VMEM((PLANE * B, R), f32),
            pltpu.VMEM((PLANE, B, R), bf16),
            pltpu.VMEM((PLANE, B, R), bf16),
            *sums, *sums, *sums,
            dma((2,)),
            dma((LINE,)),
            dma((Z,)),
            dma((2,)),
            dma((PLANE,)),
            dma((1,)),
            dma((2,)),
            dma((2,)),
            dma((6,)),
            dma((6,)),
            dma((6,)),
        ],
        compiler_params=pltpu.CompilerParams(
            collective_id=0, has_side_effects=True, vmem_limit_bytes=VMEMLIM * 1024 * 1024
        ),
    )(features, targets)
    residual = targets - taken
    return coefficients, residual, residual + added


def solution(mesh):
    spec = P(None, ("col", "row"))
    return jax.shard_map(
        local, mesh=mesh, in_specs=(spec, spec), out_specs=(spec, spec, spec), check_vma=False
    )
```

```python
import math

import jax
import jax.numpy as jnp
from jax import lax
from jax.experimental import pallas as pl
from jax.experimental.pallas import tpu as pltpu
from jax.sharding import PartitionSpec as P

F = 64
R = 128
B = 128
X, Y, Z, C = 4, 4, 8, 2
PLANE = X * Y
LINE = Z * C
EARLY = 5
VMEMLIM = 40

ridge_weight = 0.5
kernel_gain = 2.0
sharpness = 3.0
exponent_scale = sharpness / F * math.log2(math.e)

f32 = jnp.float32
bf16 = jnp.bfloat16


def dot_exact(left, right):
    return jnp.dot(left, right, precision=lax.Precision.HIGHEST, preferred_element_type=f32)


def norm_rows(feat, rows):
    wide = feat.astype(f32)
    total = jnp.sum(wide * wide, axis=0, keepdims=True)
    high = total.astype(bf16).astype(f32)
    mid = (total - high).astype(bf16).astype(f32)
    low = (total - high - mid).astype(bf16).astype(f32)
    width = feat.shape[1]
    index = lax.broadcasted_iota(jnp.int32, (F, width), 0)
    first = 0 if rows else 3
    other = 3 if rows else 0
    sign = 1.0 if rows else -1.0
    extra = jnp.where(index == first, sign * high, 0.0)
    extra = jnp.where(index == first + 1, sign * mid, extra)
    extra = jnp.where(index == first + 2, sign * low, extra)
    extra = jnp.where((index >= other) & (index < other + 3), sign, extra)
    scaled = wide if rows else 2.0 * wide
    return jnp.concatenate([scaled, extra], axis=0)


def sweep_inverse(matrix):
    lanes = lax.broadcasted_iota(jnp.int32, (8, R), 1)
    subs = lax.broadcasted_iota(jnp.int32, (8, R), 0)

    def spread_lane(tile, lane):
        return jnp.broadcast_to(tile[:, lane : lane + 1], (8, R))

    def spread_line(tile, sub):
        return jnp.broadcast_to(tile[sub : sub + 1, :], (8, R))

    def eight(block, tiles):
        start = 8 * block
        own = (lanes >= start) & (lanes < start + 8)
        head = tiles[block]
        cols = [spread_lane(head, start + p) for p in range(8)]
        pivot = {(s, t): spread_line(cols[t], s) for t in range(8) for s in range(t + 1)}
        rows = [jnp.where(own, jnp.where(lanes == start + p, -1.0, 0.0), spread_line(head, p)) for p in range(8)]
        for p in range(8):
            inverse = 1.0 / pivot[p, p]
            rows[p] = rows[p] * inverse
            ahead = {t: pivot[p, t] * inverse for t in range(p + 1, 8)}
            for s in range(8):
                if s != p:
                    rows[s] = rows[s] - pivot[min(s, p), max(s, p)] * rows[p]
            for t in range(p + 1, 8):
                for s in range(t + 1):
                    if s < p:
                        pivot[s, t] = pivot[s, t] - pivot[s, p] * ahead[t]
                    elif s > p:
                        pivot[s, t] = pivot[s, t] - pivot[p, s] * ahead[t]
            for t in ahead:
                pivot[p, t] = ahead[t]
        swept = rows[7]
        for p in range(7):
            swept = jnp.where(subs == p, rows[p], swept)
        after = []
        for at, tile in enumerate(tiles):
            if at == block:
                after.append(swept)
                continue
            terms = [spread_lane(tile, start + p) * rows[p] for p in range(8)]
            while len(terms) > 1:
                terms = [terms[k] + terms[k + 1] for k in range(0, len(terms), 2)]
            after.append(jnp.where(own, 0.0, tile) - terms[0])
        return after

    tiles = [matrix[8 * t : 8 * t + 8, :] for t in range(R // 8)]
    for block in range(R // 8):
        tiles = eight(block, tiles)
    return jnp.concatenate(tiles, axis=0)


def kernel(
    feat_ref, targ_ref, coef_ref, resid_ref, change_ref,
    targ_own, block, row_feat, row_targ, row_aug, col_aug, total, outgoing, incoming,
    sq_local, sq_in, sq_sum, sq_line, sq_full,
    cu_local, cu_in, cu_sum, cu_line, cu_full,
    gr_local, gr_in, gr_sum, gr_line, gr_full,
    load_sems, block_recv, cross_send, line_send, row_recv, row_send, targ_sems, image_sems, sq_sems, cu_sems, gr_sems,
):
    row, col = lax.axis_index("row"), lax.axis_index("col")
    x, z = row // Z, row % Z
    y, core = col // C, col % C
    here = x * Y + y

    def at_plane(step):
        tx, ty = (x + step // Y) % X, (y + step % Y) % Y
        return (tx * Z + z, ty * C + core), tx * Y + ty

    def at_plane_back(step):
        tx, ty = (x + X - step // Y) % X, (y + Y - step % Y) % Y
        return (tx * Z + z, ty * C + core)

    def at_line(step):
        tz, tc = (z + step // C) % Z, (core + step % C) % C
        return (x * Z + tz, y * C + tc)

    sibling = (row, y * C + 1 - core)

    def up(step):
        return (x * Z + (z + step) % Z, col)

    def send(src, dst, send_sem, recv_sem, device):
        pltpu.make_async_remote_copy(
            src_ref=src, dst_ref=dst, send_sem=send_sem, recv_sem=recv_sem,
            device_id=device, device_id_type=pl.DeviceIdType.MESH,
        ).start()

    def take(ref, sem):
        pltpu.make_async_copy(ref, ref, sem).wait()

    barrier = pltpu.get_barrier_semaphore()

    def greet(step, carry):
        pl.semaphore_signal(barrier, inc=1, device_id=at_plane(step)[0], device_id_type=pl.DeviceIdType.MESH)
        pl.semaphore_signal(barrier, inc=1, device_id=at_line(step), device_id_type=pl.DeviceIdType.MESH)
        return carry

    lax.fori_loop(1, PLANE, greet, 0)

    load_feat = pltpu.make_async_copy(feat_ref, block.at[0, pl.ds(0, F)], load_sems.at[0])
    load_targ = pltpu.make_async_copy(targ_ref, targ_own, load_sems.at[1])
    load_targ.start()
    load_feat.start()
    load_targ.wait()
    load_feat.wait()
    targ = targ_own[...]
    targ_t = targ.T
    targ_high = targ.astype(bf16)
    row_targ[0] = targ_high
    block[0, F : F + R, :] = targ_t.astype(bf16)
    pl.semaphore_wait(barrier, PLANE + LINE - 2)

    def order(step):
        return jnp.where(step % 2 == 1, (step + 1) // 2, (Z - step // 2) % Z)

    def across(slot):
        send(block.at[slot], block.at[slot + Z], cross_send.at[slot], block_recv.at[slot + Z], sibling)

    def send_block(slot):
        send(block.at[0], block.at[slot], line_send.at[0], block_recv.at[slot], up(slot))

    def plane_order(step):
        turn = step // Y
        return (turn + turn // 2 - 2 * (turn // 3)) * Y + step % Y

    def send_feat(step, carry):
        slot = plane_order(PLANE - step)
        send(block.at[0, pl.ds(0, F)], row_feat.at[slot], row_send.at[0], row_recv.at[slot], at_plane(slot)[0])
        return carry

    def send_targ(step, carry):
        send(row_targ.at[0], row_targ.at[step], targ_sems.at[0], targ_sems.at[1], at_plane(step)[0])
        return carry

    for slot in (2, Z - 2, 1, Z - 1):
        send_block(slot)
    lax.fori_loop(1, PLANE, send_feat, 0)
    across(0)

    def reduce_plane(local, arrive, sems):
        def one(step, carry):
            device, piece = at_plane(step)
            send(local.at[piece], arrive.at[step - 1], sems.at[0], sems.at[1], device)
            return carry

        lax.fori_loop(1, PLANE, one, 0)

    def sum_line(local, arrive, own, line, sems):
        take(arrive, sems.at[1])
        own[...] = local[here] + jnp.sum(arrive[...], axis=0)

        def one(step, carry):
            send(own, line.at[step - 1], sems.at[2], sems.at[3], at_line(step))
            return carry

        lax.fori_loop(1, LINE, one, 0)

    def spread_plane(own, line, full, sems):
        take(line, sems.at[3])
        full[here] = own[...] + jnp.sum(line[...], axis=0)

        def one(step, carry):
            send(full.at[here], full.at[here], sems.at[4], sems.at[5], at_plane(step)[0])
            return carry

        lax.fori_loop(1, PLANE, one, 0)

    def finish(arrive, sems):
        take(arrive, sems.at[5])

    def settle(arrive, line, sems):
        take(arrive, sems.at[0])
        take(line, sems.at[2])
        take(arrive, sems.at[4])

    sq_local[...] = dot_exact(targ, targ_t).reshape(PLANE, 8, R)
    reduce_plane(sq_local, sq_in, sq_sems)
    lax.fori_loop(1, PLANE, send_targ, 0)
    row_aug[0:B, :] = norm_rows(block[0, 0:F, :], True).T.astype(bf16)

    def arrived(slot):
        take(block.at[slot], block_recv.at[slot])

    def pass_on(step, carry):
        arrived(order(step))
        across(order(step))
        return carry


    def augment(step, carry):
        slot = plane_order(step)
        take(row_feat.at[slot], row_recv.at[slot])
        row_aug[pl.ds(pl.multiple_of(slot * B, B), B), :] = norm_rows(row_feat[slot], True).T.astype(bf16)
        return carry


    def columns(pair):
        arrived(pair + Z)
        feats = jnp.concatenate([block[pair, 0:F, :], block[pair + Z, 0:F, :]], axis=1)
        col_aug[pair] = norm_rows(feats, False).astype(bf16)

    def product(rows, pair):
        minus = jnp.dot(rows, col_aug[pair], preferred_element_type=f32)
        entries = jnp.exp2(minus * exponent_scale).astype(bf16)
        panel = jnp.concatenate([block[pair, F : F + R, :], block[pair + Z, F : F + R, :]], axis=0)
        return jnp.dot(entries, panel, preferred_element_type=f32)

    def rows_times(first, pairs, fresh):
        where = pl.ds(first * B, PLANE // 2 * B)
        rows = row_aug[where, :]
        value = None if fresh else total[where, :]
        for pair in pairs:
            term = product(rows, pair)
            value = term if value is None else value + term
        total[where, :] = value

    half = (F + R) // 2
    for slot, direction, first in ((2, 1, 0), (Z - 2, Z - 1, half)):
        arrived(slot)
        to = (slot + direction) % Z
        send(block.at[slot], block.at[to], line_send.at[1], block_recv.at[to], up(direction))
        rows = pl.ds(first, half)
        send(block.at[slot, rows], block.at[4, rows], line_send.at[1], block_recv.at[4], up(slot))
        across(slot)
    lax.fori_loop(1, 3, pass_on, 0)
    lax.fori_loop(1, PLANE // 2, augment, 0)
    near = (0, 1, Z - 1)
    for pair in near:
        columns(pair)
    rows_times(0, near, True)
    lax.fori_loop(PLANE // 2, PLANE, augment, 0)
    lax.fori_loop(EARLY, Z - 1, pass_on, 0)
    rows_times(PLANE // 2, near, True)
    lax.fori_loop(Z - 1, Z, pass_on, 0)
    for pair in (2, Z - 2):
        columns(pair)
        total[...] += product(row_aug[...], pair)
    sum_line(sq_local, sq_in, sq_sum, sq_line, sq_sems)
    last = [(step + 1) // 2 if step % 2 else Z - step // 2 for step in range(EARLY, Z)]
    for pair in last:
        columns(pair)

    def part(dx):
        where = pl.ds(pl.multiple_of(dx * Y * B, Y * B), Y * B)
        rows = row_aug[where, :]
        value = total[where, :]
        for pair in last:
            value = value + product(rows, pair)
        return value

    def send_rows(slot):
        send(outgoing.at[slot], incoming.at[slot], image_sems.at[0], image_sems.at[1], at_plane_back(slot))

    def finish_rows(step, carry):
        dx = 2 + step - 3 * (step // 2)
        outgoing[pl.ds(dx * Y, Y)] = part(dx).astype(bf16).reshape(Y, B, R)


        @pl.when(step < 2)
        def _():
            send_group(dx)

        return carry

    def send_group(dx):
        for dy in (2, 1, 3, 0):
            send_rows(dx * Y + dy)

    lax.fori_loop(0, X - 1, finish_rows, 0)
    own = part(0)
    outgoing[pl.ds(1, Y - 1)] = own[B:, :].astype(bf16).reshape(Y - 1, B, R)
    own = own[0:B, :]
    row_targs = row_targ.at[pl.ds(1, PLANE - 1)]
    take(row_targs, targ_sems.at[1])
    targs = jnp.concatenate([row_targ[slot] for slot in range(1, PLANE)], axis=1)
    images = outgoing[pl.ds(1, PLANE - 1)].reshape((PLANE - 1) * B, R)
    term = dot_exact(targ, own) + jnp.dot(targs, images, preferred_element_type=f32)
    cu_local[...] = ridge_weight * sq_local[...] + kernel_gain * term.reshape(PLANE, 8, R)
    reduce_plane(cu_local, cu_in, cu_sems)
    send_group(1)
    for dy in (2, 1, 3):
        send_rows(dy)

    sum_line(cu_local, cu_in, cu_sum, cu_line, cu_sems)
    others = incoming.at[pl.ds(1, PLANE - 1)]
    take(others, image_sems.at[1])

    kernel_image_t = own
    for slot in range(1, PLANE):
        kernel_image_t = kernel_image_t + incoming[slot].astype(f32)
    image_t = ridge_weight * targ_t + kernel_gain * kernel_image_t
    image = image_t.T
    gr_local[...] = dot_exact(image, image_t).reshape(PLANE, 8, R)
    reduce_plane(gr_local, gr_in, gr_sems)
    spread_plane(sq_sum, sq_line, sq_full, sq_sems)
    spread_plane(cu_sum, cu_line, cu_full, cu_sems)
    sum_line(gr_local, gr_in, gr_sum, gr_line, gr_sems)
    spread_plane(gr_sum, gr_line, gr_full, gr_sems)

    finish(cu_in, cu_sems)
    curvature = cu_full[...].reshape(R, R)
    curvature_t = curvature.T
    minus_inverse = sweep_inverse(0.5 * (curvature + curvature_t))
    finish(sq_in, sq_sems)
    squares = sq_full[...].reshape(R, R)
    step_size = -dot_exact(minus_inverse, squares)
    step_t = step_size.T
    coef_ref[...] = dot_exact(step_t, targ)
    residual = targ - dot_exact(step_t, image)
    resid_ref[...] = residual
    solved = dot_exact(minus_inverse, targ)
    before = dot_exact(curvature, solved)
    finish(gr_in, gr_sems)
    image_gram = gr_full[...].reshape(R, R)
    change_ref[...] = before - dot_exact(step_t, dot_exact(image_gram, solved))

    take(row_feat.at[pl.ds(1, PLANE - 1)], row_send.at[0])
    take(row_targs, targ_sems.at[0])
    take(others, image_sems.at[0])
    settle(sq_in, sq_line, sq_sems)
    settle(cu_in, cu_line, cu_sems)
    settle(gr_in, gr_line, gr_sems)
    take(block.at[pl.ds(1, 4)], line_send.at[0])
    take(block.at[pl.ds(1, 3)], line_send.at[1])
    for slot in range(Z):
        take(block.at[slot], cross_send.at[slot])


def place(coef_ref, resid_ref, change_ref, coef_out, resid_out, dir_out):
    coef_out[...] = coef_ref[...]
    residual = resid_ref[...]
    resid_out[...] = residual
    dir_out[...] = residual + change_ref[...]


def local(features, targets):
    whole = jax.ShapeDtypeStruct((R, B), f32)
    vmem = pl.BlockSpec(memory_space=pltpu.VMEM)
    hbm = pl.BlockSpec(memory_space=pltpu.HBM)
    dma = pltpu.SemaphoreType.DMA
    sums = [
        pltpu.VMEM((PLANE, 8, R), f32),
        pltpu.VMEM((PLANE - 1, 8, R), f32),
        pltpu.VMEM((8, R), f32),
        pltpu.VMEM((LINE - 1, 8, R), f32),
        pltpu.VMEM((PLANE, 8, R), f32),
    ]
    results = pl.pallas_call(
        kernel,
        out_shape=(whole, whole, whole),
        in_specs=[hbm, hbm],
        out_specs=(vmem, vmem, vmem),
        scratch_shapes=[
            pltpu.VMEM((R, B), f32),
            pltpu.VMEM((LINE, F + R, B), bf16),
            pltpu.VMEM((PLANE, F, B), bf16),
            pltpu.VMEM((PLANE, R, B), bf16),
            pltpu.VMEM((PLANE * B, 2 * F), bf16),
            pltpu.VMEM((LINE // 2, 2 * F, 2 * B), bf16),
            pltpu.VMEM((PLANE * B, R), f32),
            pltpu.VMEM((PLANE, B, R), bf16),
            pltpu.VMEM((PLANE, B, R), bf16),
            *sums, *sums, *sums,
            dma((2,)),
            dma((LINE,)),
            dma((Z,)),
            dma((2,)),
            dma((PLANE,)),
            dma((1,)),
            dma((2,)),
            dma((2,)),
            dma((6,)),
            dma((6,)),
            dma((6,)),
        ],
        compiler_params=pltpu.CompilerParams(
            collective_id=0, has_side_effects=True, vmem_limit_bytes=VMEMLIM * 1024 * 1024
        ),
    )(features, targets)
    return pl.pallas_call(
        place,
        out_shape=(whole, whole, whole),
        in_specs=[vmem] * 3,
        out_specs=(vmem, vmem, vmem),
        compiler_params=pltpu.CompilerParams(vmem_limit_bytes=2 * 1024 * 1024),
    )(*results)


def solution(mesh):
    spec = P(None, ("col", "row"))
    return jax.shard_map(
        local, mesh=mesh, in_specs=(spec, spec), out_specs=(spec, spec, spec), check_vma=False
    )
```

```python
import math

import jax
import jax.numpy as jnp
from jax import lax
from jax.experimental import pallas as pl
from jax.experimental.pallas import tpu as pltpu
from jax.sharding import PartitionSpec as P

F = 64
R = 128
B = 128
X, Y, Z, C = 4, 4, 8, 2
PLANE = X * Y
LINE = Z * C
EARLY = 5
VMEMLIM = 40

ridge_weight = 0.5
kernel_gain = 2.0
sharpness = 3.0
exponent_scale = sharpness / F * math.log2(math.e)

f32 = jnp.float32
bf16 = jnp.bfloat16


def dot_exact(left, right):
    return jnp.dot(left, right, precision=lax.Precision.HIGHEST, preferred_element_type=f32)


def norm_rows(feat, rows):
    wide = feat.astype(f32)
    total = jnp.sum(wide * wide, axis=0, keepdims=True)
    high = total.astype(bf16).astype(f32)
    mid = (total - high).astype(bf16).astype(f32)
    low = (total - high - mid).astype(bf16).astype(f32)
    width = feat.shape[1]
    index = lax.broadcasted_iota(jnp.int32, (F, width), 0)
    first = 0 if rows else 3
    other = 3 if rows else 0
    sign = 1.0 if rows else -1.0
    extra = jnp.where(index == first, sign * high, 0.0)
    extra = jnp.where(index == first + 1, sign * mid, extra)
    extra = jnp.where(index == first + 2, sign * low, extra)
    extra = jnp.where((index >= other) & (index < other + 3), sign, extra)
    scaled = wide if rows else 2.0 * wide
    return jnp.concatenate([scaled, extra], axis=0)


def sweep_inverse(matrix):
    lanes = lax.broadcasted_iota(jnp.int32, (8, R), 1)
    subs = lax.broadcasted_iota(jnp.int32, (8, R), 0)

    def spread_lane(tile, lane):
        return jnp.broadcast_to(tile[:, lane : lane + 1], (8, R))

    def spread_line(tile, sub):
        return jnp.broadcast_to(tile[sub : sub + 1, :], (8, R))

    def eight(block, tiles):
        start = 8 * block
        own = (lanes >= start) & (lanes < start + 8)
        head = tiles[block]
        cols = [spread_lane(head, start + p) for p in range(8)]
        pivot = {(s, t): spread_line(cols[t], s) for t in range(8) for s in range(t + 1)}
        rows = [jnp.where(own, jnp.where(lanes == start + p, -1.0, 0.0), spread_line(head, p)) for p in range(8)]
        for p in range(8):
            inverse = 1.0 / pivot[p, p]
            rows[p] = rows[p] * inverse
            ahead = {t: pivot[p, t] * inverse for t in range(p + 1, 8)}
            for s in range(8):
                if s != p:
                    rows[s] = rows[s] - pivot[min(s, p), max(s, p)] * rows[p]
            for t in range(p + 1, 8):
                for s in range(t + 1):
                    if s < p:
                        pivot[s, t] = pivot[s, t] - pivot[s, p] * ahead[t]
                    elif s > p:
                        pivot[s, t] = pivot[s, t] - pivot[p, s] * ahead[t]
            for t in ahead:
                pivot[p, t] = ahead[t]
        swept = rows[7]
        for p in range(7):
            swept = jnp.where(subs == p, rows[p], swept)
        after = []
        for at, tile in enumerate(tiles):
            if at == block:
                after.append(swept)
                continue
            terms = [spread_lane(tile, start + p) * rows[p] for p in range(8)]
            while len(terms) > 1:
                terms = [terms[k] + terms[k + 1] for k in range(0, len(terms), 2)]
            after.append(jnp.where(own, 0.0, tile) - terms[0])
        return after

    tiles = [matrix[8 * t : 8 * t + 8, :] for t in range(R // 8)]
    for block in range(R // 8):
        tiles = eight(block, tiles)
    return jnp.concatenate(tiles, axis=0)


def kernel(
    feat_ref, targ_ref, coef_ref, resid_ref, change_ref,
    block, row_feat, row_targ, row_aug, col_aug, total, outgoing, incoming,
    sq_local, sq_in, sq_sum, sq_line, sq_full,
    cu_local, cu_in, cu_sum, cu_line, cu_full,
    gr_local, gr_in, gr_sum, gr_line, gr_full,
    block_recv, cross_send, line_send, row_recv, row_send, targ_sems, image_sems, sq_sems, cu_sems, gr_sems,
):
    row, col = lax.axis_index("row"), lax.axis_index("col")
    x, z = row // Z, row % Z
    y, core = col // C, col % C
    here = x * Y + y

    def at_plane(step):
        tx, ty = (x + step // Y) % X, (y + step % Y) % Y
        return (tx * Z + z, ty * C + core), tx * Y + ty

    def at_plane_back(step):
        tx, ty = (x + X - step // Y) % X, (y + Y - step % Y) % Y
        return (tx * Z + z, ty * C + core)

    def at_line(step):
        tz, tc = (z + step // C) % Z, (core + step % C) % C
        return (x * Z + tz, y * C + tc)

    sibling = (row, y * C + 1 - core)

    def up(step):
        return (x * Z + (z + step) % Z, col)

    def send(src, dst, send_sem, recv_sem, device):
        pltpu.make_async_remote_copy(
            src_ref=src, dst_ref=dst, send_sem=send_sem, recv_sem=recv_sem,
            device_id=device, device_id_type=pl.DeviceIdType.MESH,
        ).start()

    def take(ref, sem):
        pltpu.make_async_copy(ref, ref, sem).wait()

    barrier = pltpu.get_barrier_semaphore()

    def greet(step, carry):
        pl.semaphore_signal(barrier, inc=1, device_id=at_plane(step)[0], device_id_type=pl.DeviceIdType.MESH)
        pl.semaphore_signal(barrier, inc=1, device_id=at_line(step), device_id_type=pl.DeviceIdType.MESH)
        return carry

    lax.fori_loop(1, PLANE, greet, 0)

    block[0, 0:F, :] = feat_ref[...]
    targ = targ_ref[...]
    targ_t = targ.T
    targ_high = targ.astype(bf16)
    row_targ[0] = targ_high
    block[0, F : F + R, :] = targ_t.astype(bf16)
    pl.semaphore_wait(barrier, PLANE + LINE - 2)

    def order(step):
        return jnp.where(step % 2 == 1, (step + 1) // 2, (Z - step // 2) % Z)

    def across(slot):
        send(block.at[slot], block.at[slot + Z], cross_send.at[slot], block_recv.at[slot + Z], sibling)

    def send_block(slot):
        send(block.at[0], block.at[slot], line_send.at[0], block_recv.at[slot], up(slot))

    def plane_order(step):
        turn = step // Y
        return (turn + turn // 2 - 2 * (turn // 3)) * Y + step % Y

    def send_feat(step, carry):
        slot = plane_order(PLANE - step)
        send(block.at[0, pl.ds(0, F)], row_feat.at[slot], row_send.at[0], row_recv.at[slot], at_plane(slot)[0])
        return carry

    def send_targ(step, carry):
        send(row_targ.at[0], row_targ.at[step], targ_sems.at[0], targ_sems.at[1], at_plane(step)[0])
        return carry

    for slot in (2, Z - 2, 1, Z - 1):
        send_block(slot)
    lax.fori_loop(1, PLANE, send_feat, 0)
    across(0)

    def reduce_plane(local, arrive, sems):
        def one(step, carry):
            device, piece = at_plane(step)
            send(local.at[piece], arrive.at[step - 1], sems.at[0], sems.at[1], device)
            return carry

        lax.fori_loop(1, PLANE, one, 0)

    def sum_line(local, arrive, own, line, sems):
        take(arrive, sems.at[1])
        own[...] = local[here] + jnp.sum(arrive[...], axis=0)

        def one(step, carry):
            send(own, line.at[step - 1], sems.at[2], sems.at[3], at_line(step))
            return carry

        lax.fori_loop(1, LINE, one, 0)

    def spread_plane(own, line, full, sems):
        take(line, sems.at[3])
        full[here] = own[...] + jnp.sum(line[...], axis=0)

        def one(step, carry):
            send(full.at[here], full.at[here], sems.at[4], sems.at[5], at_plane(step)[0])
            return carry

        lax.fori_loop(1, PLANE, one, 0)

    def finish(arrive, sems):
        take(arrive, sems.at[5])

    def settle(arrive, line, sems):
        take(arrive, sems.at[0])
        take(line, sems.at[2])
        take(arrive, sems.at[4])

    sq_local[...] = dot_exact(targ, targ_t).reshape(PLANE, 8, R)
    reduce_plane(sq_local, sq_in, sq_sems)
    lax.fori_loop(1, PLANE, send_targ, 0)
    row_aug[0:B, :] = norm_rows(block[0, 0:F, :], True).T.astype(bf16)

    def arrived(slot):
        take(block.at[slot], block_recv.at[slot])

    def pass_on(step, carry):
        arrived(order(step))
        across(order(step))
        return carry


    def augment(step, carry):
        slot = plane_order(step)
        take(row_feat.at[slot], row_recv.at[slot])
        row_aug[pl.ds(pl.multiple_of(slot * B, B), B), :] = norm_rows(row_feat[slot], True).T.astype(bf16)
        return carry


    def columns(pair):
        arrived(pair + Z)
        feats = jnp.concatenate([block[pair, 0:F, :], block[pair + Z, 0:F, :]], axis=1)
        col_aug[pair] = norm_rows(feats, False).astype(bf16)

    def product(rows, pair):
        minus = jnp.dot(rows, col_aug[pair], preferred_element_type=f32)
        entries = jnp.exp2(minus * exponent_scale).astype(bf16)
        panel = jnp.concatenate([block[pair, F : F + R, :], block[pair + Z, F : F + R, :]], axis=0)
        return jnp.dot(entries, panel, preferred_element_type=f32)

    def rows_times(first, pairs, fresh):
        where = pl.ds(first * B, PLANE // 2 * B)
        rows = row_aug[where, :]
        value = None if fresh else total[where, :]
        for pair in pairs:
            term = product(rows, pair)
            value = term if value is None else value + term
        total[where, :] = value

    half = (F + R) // 2
    for slot, direction, first in ((2, 1, 0), (Z - 2, Z - 1, half)):
        arrived(slot)
        to = (slot + direction) % Z
        send(block.at[slot], block.at[to], line_send.at[1], block_recv.at[to], up(direction))
        rows = pl.ds(first, half)
        send(block.at[slot, rows], block.at[4, rows], line_send.at[1], block_recv.at[4], up(slot))
        across(slot)
    lax.fori_loop(1, 3, pass_on, 0)
    lax.fori_loop(1, PLANE // 2, augment, 0)
    near = (0, 1, Z - 1)
    for pair in near:
        columns(pair)
    rows_times(0, near, True)
    lax.fori_loop(PLANE // 2, PLANE, augment, 0)
    lax.fori_loop(EARLY, Z - 1, pass_on, 0)
    rows_times(PLANE // 2, near, True)
    lax.fori_loop(Z - 1, Z, pass_on, 0)
    for pair in (2, Z - 2):
        columns(pair)
        total[...] += product(row_aug[...], pair)
    sum_line(sq_local, sq_in, sq_sum, sq_line, sq_sems)
    last = [(step + 1) // 2 if step % 2 else Z - step // 2 for step in range(EARLY, Z)]
    for pair in last:
        columns(pair)

    def part(first):
        where = pl.ds(first * B, PLANE // 2 * B)
        rows = row_aug[where, :]
        value = total[where, :]
        for pair in last:
            value = value + product(rows, pair)
        return value

    def send_rows(slot):
        send(outgoing.at[slot], incoming.at[slot], image_sems.at[0], image_sems.at[1], at_plane_back(slot))

    def send_group(dx):
        for dy in (2, 1, 3, 0):
            send_rows(dx * Y + dy)

    outgoing[PLANE // 2 :] = part(PLANE // 2).astype(bf16).reshape(PLANE // 2, B, R)
    send_group(2)
    send_group(3)
    own = part(0)
    outgoing[1 : PLANE // 2] = own[B:, :].astype(bf16).reshape(PLANE // 2 - 1, B, R)
    own = own[0:B, :]
    row_targs = row_targ.at[pl.ds(1, PLANE - 1)]
    take(row_targs, targ_sems.at[1])
    targs = jnp.concatenate([row_targ[slot] for slot in range(1, PLANE)], axis=1)
    images = outgoing[pl.ds(1, PLANE - 1)].reshape((PLANE - 1) * B, R)
    term = dot_exact(targ, own) + jnp.dot(targs, images, preferred_element_type=f32)
    cu_local[...] = ridge_weight * sq_local[...] + kernel_gain * term.reshape(PLANE, 8, R)
    reduce_plane(cu_local, cu_in, cu_sems)
    send_group(1)
    for dy in (2, 1, 3):
        send_rows(dy)

    sum_line(cu_local, cu_in, cu_sum, cu_line, cu_sems)
    others = incoming.at[pl.ds(1, PLANE - 1)]
    take(others, image_sems.at[1])

    kernel_image_t = own
    for slot in range(1, PLANE):
        kernel_image_t = kernel_image_t + incoming[slot].astype(f32)
    image_t = ridge_weight * targ_t + kernel_gain * kernel_image_t
    image = image_t.T
    gr_local[...] = dot_exact(image, image_t).reshape(PLANE, 8, R)
    reduce_plane(gr_local, gr_in, gr_sems)
    spread_plane(sq_sum, sq_line, sq_full, sq_sems)
    spread_plane(cu_sum, cu_line, cu_full, cu_sems)
    sum_line(gr_local, gr_in, gr_sum, gr_line, gr_sems)
    spread_plane(gr_sum, gr_line, gr_full, gr_sems)

    finish(cu_in, cu_sems)
    curvature = cu_full[...].reshape(R, R)
    curvature_t = curvature.T
    minus_inverse = sweep_inverse(0.5 * (curvature + curvature_t))
    finish(sq_in, sq_sems)
    squares = sq_full[...].reshape(R, R)
    step_size = -dot_exact(minus_inverse, squares)
    step_t = step_size.T
    coef_ref[...] = dot_exact(step_t, targ)
    residual = targ - dot_exact(step_t, image)
    resid_ref[...] = residual
    solved = dot_exact(minus_inverse, targ)
    before = dot_exact(curvature, solved)
    finish(gr_in, gr_sems)
    image_gram = gr_full[...].reshape(R, R)
    change_ref[...] = before - dot_exact(step_t, dot_exact(image_gram, solved))

    take(row_feat.at[pl.ds(1, PLANE - 1)], row_send.at[0])
    take(row_targs, targ_sems.at[0])
    take(others, image_sems.at[0])
    settle(sq_in, sq_line, sq_sems)
    settle(cu_in, cu_line, cu_sems)
    settle(gr_in, gr_line, gr_sems)
    take(block.at[pl.ds(1, 4)], line_send.at[0])
    take(block.at[pl.ds(1, 3)], line_send.at[1])
    for slot in range(Z):
        take(block.at[slot], cross_send.at[slot])


def place(coef_ref, resid_ref, change_ref, coef_out, resid_out, dir_out):
    coef_out[...] = coef_ref[...]
    residual = resid_ref[...]
    resid_out[...] = residual
    dir_out[...] = residual + change_ref[...]


def local(features, targets):
    whole = jax.ShapeDtypeStruct((R, B), f32)
    vmem = pl.BlockSpec(memory_space=pltpu.VMEM)
    dma = pltpu.SemaphoreType.DMA
    sums = [
        pltpu.VMEM((PLANE, 8, R), f32),
        pltpu.VMEM((PLANE - 1, 8, R), f32),
        pltpu.VMEM((8, R), f32),
        pltpu.VMEM((LINE - 1, 8, R), f32),
        pltpu.VMEM((PLANE, 8, R), f32),
    ]
    results = pl.pallas_call(
        kernel,
        out_shape=(whole, whole, whole),
        in_specs=[vmem, vmem],
        out_specs=(vmem, vmem, vmem),
        scratch_shapes=[
            pltpu.VMEM((LINE, F + R, B), bf16),
            pltpu.VMEM((PLANE, F, B), bf16),
            pltpu.VMEM((PLANE, R, B), bf16),
            pltpu.VMEM((PLANE * B, 2 * F), bf16),
            pltpu.VMEM((LINE // 2, 2 * F, 2 * B), bf16),
            pltpu.VMEM((PLANE * B, R), f32),
            pltpu.VMEM((PLANE, B, R), bf16),
            pltpu.VMEM((PLANE, B, R), bf16),
            *sums, *sums, *sums,
            dma((LINE,)),
            dma((Z,)),
            dma((2,)),
            dma((PLANE,)),
            dma((1,)),
            dma((2,)),
            dma((2,)),
            dma((6,)),
            dma((6,)),
            dma((6,)),
        ],
        compiler_params=pltpu.CompilerParams(
            collective_id=0, has_side_effects=True, vmem_limit_bytes=VMEMLIM * 1024 * 1024
        ),
    )(features, targets)
    return pl.pallas_call(
        place,
        out_shape=(whole, whole, whole),
        in_specs=[vmem] * 3,
        out_specs=(vmem, vmem, vmem),
        compiler_params=pltpu.CompilerParams(vmem_limit_bytes=2 * 1024 * 1024),
    )(*results)


def solution(mesh):
    spec = P(None, ("col", "row"))
    return jax.shard_map(
        local, mesh=mesh, in_specs=(spec, spec), out_specs=(spec, spec, spec), check_vma=False
    )
```

```python
import math

import jax
import jax.numpy as jnp
from jax import lax
from jax.experimental import pallas as pl
from jax.experimental.pallas import tpu as pltpu
from jax.sharding import PartitionSpec as P

F = 64
R = 128
B = 128
X, Y, Z, C = 4, 4, 8, 2
PLANE = X * Y
LINE = Z * C
EARLY = 5
VMEMLIM = 40

ridge_weight = 0.5
kernel_gain = 2.0
sharpness = 3.0
exponent_scale = sharpness / F * math.log2(math.e)

f32 = jnp.float32
bf16 = jnp.bfloat16


def dot_exact(left, right):
    return jnp.dot(left, right, precision=lax.Precision.HIGHEST, preferred_element_type=f32)


def norm_rows(feat, rows):
    wide = feat.astype(f32)
    total = jnp.sum(wide * wide, axis=0, keepdims=True)
    high = total.astype(bf16).astype(f32)
    mid = (total - high).astype(bf16).astype(f32)
    low = (total - high - mid).astype(bf16).astype(f32)
    width = feat.shape[1]
    index = lax.broadcasted_iota(jnp.int32, (F, width), 0)
    first = 0 if rows else 3
    other = 3 if rows else 0
    sign = 1.0 if rows else -1.0
    extra = jnp.where(index == first, sign * high, 0.0)
    extra = jnp.where(index == first + 1, sign * mid, extra)
    extra = jnp.where(index == first + 2, sign * low, extra)
    extra = jnp.where((index >= other) & (index < other + 3), sign, extra)
    scaled = wide if rows else 2.0 * wide
    return jnp.concatenate([scaled, extra], axis=0)


def sweep_inverse(matrix):
    lanes = lax.broadcasted_iota(jnp.int32, (8, R), 1)
    subs = lax.broadcasted_iota(jnp.int32, (8, R), 0)

    def spread_lane(tile, lane):
        return jnp.broadcast_to(tile[:, lane : lane + 1], (8, R))

    def spread_line(tile, sub):
        return jnp.broadcast_to(tile[sub : sub + 1, :], (8, R))

    def eight(block, tiles):
        start = 8 * block
        own = (lanes >= start) & (lanes < start + 8)
        head = tiles[block]
        cols = [spread_lane(head, start + p) for p in range(8)]
        pivot = {(s, t): spread_line(cols[t], s) for t in range(8) for s in range(t + 1)}
        rows = [jnp.where(own, jnp.where(lanes == start + p, -1.0, 0.0), spread_line(head, p)) for p in range(8)]
        for p in range(8):
            inverse = 1.0 / pivot[p, p]
            rows[p] = rows[p] * inverse
            ahead = {t: pivot[p, t] * inverse for t in range(p + 1, 8)}
            for s in range(8):
                if s != p:
                    rows[s] = rows[s] - pivot[min(s, p), max(s, p)] * rows[p]
            for t in range(p + 1, 8):
                for s in range(t + 1):
                    if s < p:
                        pivot[s, t] = pivot[s, t] - pivot[s, p] * ahead[t]
                    elif s > p:
                        pivot[s, t] = pivot[s, t] - pivot[p, s] * ahead[t]
            for t in ahead:
                pivot[p, t] = ahead[t]
        swept = rows[7]
        for p in range(7):
            swept = jnp.where(subs == p, rows[p], swept)
        after = []
        for at, tile in enumerate(tiles):
            if at == block:
                after.append(swept)
                continue
            terms = [spread_lane(tile, start + p) * rows[p] for p in range(8)]
            while len(terms) > 1:
                terms = [terms[k] + terms[k + 1] for k in range(0, len(terms), 2)]
            after.append(jnp.where(own, 0.0, tile) - terms[0])
        return after

    tiles = [matrix[8 * t : 8 * t + 8, :] for t in range(R // 8)]
    for block in range(R // 8):
        tiles = eight(block, tiles)
    return jnp.concatenate(tiles, axis=0)


def kernel(
    feat_ref, targ_ref, coef_ref, resid_ref, change_ref,
    block, row_feat, row_targ, row_aug, col_aug, total, outgoing, incoming,
    sq_local, sq_in, sq_sum, sq_line, sq_full,
    cu_local, cu_in, cu_sum, cu_line, cu_full,
    gr_local, gr_in, gr_sum, gr_line, gr_full,
    block_recv, cross_send, line_send, row_recv, row_send, targ_sems, image_sems, sq_sems, cu_sems, gr_sems,
):
    row, col = lax.axis_index("row"), lax.axis_index("col")
    x, z = row // Z, row % Z
    y, core = col // C, col % C
    here = x * Y + y

    def at_plane(step):
        tx, ty = (x + step // Y) % X, (y + step % Y) % Y
        return (tx * Z + z, ty * C + core), tx * Y + ty

    def at_plane_back(step):
        tx, ty = (x + X - step // Y) % X, (y + Y - step % Y) % Y
        return (tx * Z + z, ty * C + core)

    def at_line(step):
        tz, tc = (z + step // C) % Z, (core + step % C) % C
        return (x * Z + tz, y * C + tc)

    sibling = (row, y * C + 1 - core)

    def up(step):
        return (x * Z + (z + step) % Z, col)

    def send(src, dst, send_sem, recv_sem, device):
        pltpu.make_async_remote_copy(
            src_ref=src, dst_ref=dst, send_sem=send_sem, recv_sem=recv_sem,
            device_id=device, device_id_type=pl.DeviceIdType.MESH,
        ).start()

    def take(ref, sem):
        pltpu.make_async_copy(ref, ref, sem).wait()

    barrier = pltpu.get_barrier_semaphore()

    def greet(step, carry):
        pl.semaphore_signal(barrier, inc=1, device_id=at_plane(step)[0], device_id_type=pl.DeviceIdType.MESH)
        pl.semaphore_signal(barrier, inc=1, device_id=at_line(step), device_id_type=pl.DeviceIdType.MESH)
        return carry

    lax.fori_loop(1, PLANE, greet, 0)

    block[0, 0:F, :] = feat_ref[...]
    targ = targ_ref[...]
    targ_t = targ.T
    targ_high = targ.astype(bf16)
    row_targ[0] = targ_high
    block[0, F : F + R, :] = targ_t.astype(bf16)
    pl.semaphore_wait(barrier, PLANE + LINE - 2)

    def order(step):
        return jnp.where(step % 2 == 1, (step + 1) // 2, (Z - step // 2) % Z)

    def across(slot):
        send(block.at[slot], block.at[slot + Z], cross_send.at[slot], block_recv.at[slot + Z], sibling)

    def send_block(slot):
        send(block.at[0], block.at[slot], line_send.at[0], block_recv.at[slot], up(slot))

    def plane_order(step):
        turn = step // Y
        return (turn + turn // 2 - 2 * (turn // 3)) * Y + step % Y

    def send_feat(step, carry):
        slot = plane_order(PLANE - step)
        send(block.at[0, pl.ds(0, F)], row_feat.at[slot], row_send.at[0], row_recv.at[slot], at_plane(slot)[0])
        return carry

    def send_targ(step, carry):
        send(row_targ.at[0], row_targ.at[step], targ_sems.at[0], targ_sems.at[1], at_plane(step)[0])
        return carry

    for slot in (2, Z - 2, 1, Z - 1):
        send_block(slot)
    lax.fori_loop(1, PLANE, send_feat, 0)
    across(0)

    def reduce_plane(local, arrive, sems):
        def one(step, carry):
            device, piece = at_plane(step)
            send(local.at[piece], arrive.at[step - 1], sems.at[0], sems.at[1], device)
            return carry

        lax.fori_loop(1, PLANE, one, 0)

    def sum_line(local, arrive, own, line, sems):
        take(arrive, sems.at[1])
        own[...] = local[here] + jnp.sum(arrive[...], axis=0)

        def one(step, carry):
            send(own, line.at[step - 1], sems.at[2], sems.at[3], at_line(step))
            return carry

        lax.fori_loop(1, LINE, one, 0)

    def spread_plane(own, line, full, sems):
        take(line, sems.at[3])
        full[here] = own[...] + jnp.sum(line[...], axis=0)

        def one(step, carry):
            send(full.at[here], full.at[here], sems.at[4], sems.at[5], at_plane(step)[0])
            return carry

        lax.fori_loop(1, PLANE, one, 0)

    def finish(arrive, sems):
        take(arrive, sems.at[5])

    def settle(arrive, line, sems):
        take(arrive, sems.at[0])
        take(line, sems.at[2])
        take(arrive, sems.at[4])

    sq_local[...] = dot_exact(targ, targ_t).reshape(PLANE, 8, R)
    reduce_plane(sq_local, sq_in, sq_sems)
    lax.fori_loop(1, PLANE, send_targ, 0)
    row_aug[0:B, :] = norm_rows(block[0, 0:F, :], True).astype(bf16).T

    def arrived(slot):
        take(block.at[slot], block_recv.at[slot])

    def pass_on(step, carry):
        arrived(order(step))
        across(order(step))
        return carry


    def augment(step, carry):
        slot = plane_order(step)
        take(row_feat.at[slot], row_recv.at[slot])
        row_aug[pl.ds(pl.multiple_of(slot * B, B), B), :] = norm_rows(row_feat[slot], True).astype(bf16).T
        return carry


    def columns(pair):
        arrived(pair + Z)
        feats = jnp.concatenate([block[pair, 0:F, :], block[pair + Z, 0:F, :]], axis=1)
        col_aug[pair] = norm_rows(feats, False).astype(bf16)

    def product(rows, pair):
        minus = jnp.dot(rows, col_aug[pair], preferred_element_type=f32)
        entries = jnp.exp2(minus * exponent_scale).astype(bf16)
        panel = jnp.concatenate([block[pair, F : F + R, :], block[pair + Z, F : F + R, :]], axis=0)
        return jnp.dot(entries, panel, preferred_element_type=f32)

    def rows_times(first, pairs, fresh):
        where = pl.ds(first * B, PLANE // 2 * B)
        rows = row_aug[where, :]
        value = None if fresh else total[where, :]
        for pair in pairs:
            term = product(rows, pair)
            value = term if value is None else value + term
        total[where, :] = value

    half = (F + R) // 2
    for slot, direction, first in ((2, 1, 0), (Z - 2, Z - 1, half)):
        arrived(slot)
        to = (slot + direction) % Z
        send(block.at[slot], block.at[to], line_send.at[1], block_recv.at[to], up(direction))
        rows = pl.ds(first, half)
        send(block.at[slot, rows], block.at[4, rows], line_send.at[1], block_recv.at[4], up(slot))
        across(slot)
    lax.fori_loop(1, 3, pass_on, 0)
    lax.fori_loop(1, PLANE // 2, augment, 0)
    near = (0, 1, Z - 1)
    for pair in near:
        columns(pair)
    rows_times(0, near, True)
    lax.fori_loop(PLANE // 2, PLANE, augment, 0)
    lax.fori_loop(EARLY, Z - 1, pass_on, 0)
    rows_times(PLANE // 2, near, True)
    lax.fori_loop(Z - 1, Z, pass_on, 0)
    for pair in (2, Z - 2):
        columns(pair)
        total[...] += product(row_aug[...], pair)
    sum_line(sq_local, sq_in, sq_sum, sq_line, sq_sems)
    last = [(step + 1) // 2 if step % 2 else Z - step // 2 for step in range(EARLY, Z)]
    for pair in last:
        columns(pair)

    def part(first):
        where = pl.ds(first * B, PLANE // 2 * B)
        rows = row_aug[where, :]
        value = total[where, :]
        for pair in last:
            value = value + product(rows, pair)
        return value

    def send_rows(slot):
        send(outgoing.at[slot], incoming.at[slot], image_sems.at[0], image_sems.at[1], at_plane_back(slot))

    def send_group(dx):
        for dy in (2, 1, 3, 0):
            send_rows(dx * Y + dy)

    outgoing[PLANE // 2 :] = part(PLANE // 2).astype(bf16).reshape(PLANE // 2, B, R)
    send_group(2)
    send_group(3)
    own = part(0)
    outgoing[1 : PLANE // 2] = own[B:, :].astype(bf16).reshape(PLANE // 2 - 1, B, R)
    own = own[0:B, :]
    row_targs = row_targ.at[pl.ds(1, PLANE - 1)]
    take(row_targs, targ_sems.at[1])
    targs = jnp.concatenate([row_targ[slot] for slot in range(1, PLANE)], axis=1)
    images = outgoing[pl.ds(1, PLANE - 1)].reshape((PLANE - 1) * B, R)
    term = dot_exact(targ, own) + jnp.dot(targs, images, preferred_element_type=f32)
    cu_local[...] = ridge_weight * sq_local[...] + kernel_gain * term.reshape(PLANE, 8, R)
    reduce_plane(cu_local, cu_in, cu_sems)
    send_group(1)
    for dy in (2, 1, 3):
        send_rows(dy)

    sum_line(cu_local, cu_in, cu_sum, cu_line, cu_sems)
    others = incoming.at[pl.ds(1, PLANE - 1)]
    take(others, image_sems.at[1])

    kernel_image_t = own
    for slot in range(1, PLANE):
        kernel_image_t = kernel_image_t + incoming[slot].astype(f32)
    image_t = ridge_weight * targ_t + kernel_gain * kernel_image_t
    image = image_t.T
    gr_local[...] = dot_exact(image, image_t).reshape(PLANE, 8, R)
    reduce_plane(gr_local, gr_in, gr_sems)
    spread_plane(sq_sum, sq_line, sq_full, sq_sems)
    spread_plane(cu_sum, cu_line, cu_full, cu_sems)
    sum_line(gr_local, gr_in, gr_sum, gr_line, gr_sems)
    spread_plane(gr_sum, gr_line, gr_full, gr_sems)

    finish(cu_in, cu_sems)
    curvature = cu_full[...].reshape(R, R)
    curvature_t = curvature.T
    minus_inverse = sweep_inverse(0.5 * (curvature + curvature_t))
    finish(sq_in, sq_sems)
    squares = sq_full[...].reshape(R, R)
    step_size = -dot_exact(minus_inverse, squares)
    step_t = step_size.T
    coef_ref[...] = dot_exact(step_t, targ)
    residual = targ - dot_exact(step_t, image)
    resid_ref[...] = residual
    solved = dot_exact(minus_inverse, targ)
    before = dot_exact(curvature, solved)
    finish(gr_in, gr_sems)
    image_gram = gr_full[...].reshape(R, R)
    change_ref[...] = before - dot_exact(step_t, dot_exact(image_gram, solved))

    take(row_feat.at[pl.ds(1, PLANE - 1)], row_send.at[0])
    take(row_targs, targ_sems.at[0])
    take(others, image_sems.at[0])
    settle(sq_in, sq_line, sq_sems)
    settle(cu_in, cu_line, cu_sems)
    settle(gr_in, gr_line, gr_sems)
    take(block.at[pl.ds(1, 4)], line_send.at[0])
    take(block.at[pl.ds(1, 3)], line_send.at[1])
    for slot in range(Z):
        take(block.at[slot], cross_send.at[slot])


def place(coef_ref, resid_ref, change_ref, coef_out, resid_out, dir_out):
    coef_out[...] = coef_ref[...]
    residual = resid_ref[...]
    resid_out[...] = residual
    dir_out[...] = residual + change_ref[...]


def local(features, targets):
    whole = jax.ShapeDtypeStruct((R, B), f32)
    vmem = pl.BlockSpec(memory_space=pltpu.VMEM)
    dma = pltpu.SemaphoreType.DMA
    sums = [
        pltpu.VMEM((PLANE, 8, R), f32),
        pltpu.VMEM((PLANE - 1, 8, R), f32),
        pltpu.VMEM((8, R), f32),
        pltpu.VMEM((LINE - 1, 8, R), f32),
        pltpu.VMEM((PLANE, 8, R), f32),
    ]
    results = pl.pallas_call(
        kernel,
        out_shape=(whole, whole, whole),
        in_specs=[vmem, vmem],
        out_specs=(vmem, vmem, vmem),
        scratch_shapes=[
            pltpu.VMEM((LINE, F + R, B), bf16),
            pltpu.VMEM((PLANE, F, B), bf16),
            pltpu.VMEM((PLANE, R, B), bf16),
            pltpu.VMEM((PLANE * B, 2 * F), bf16),
            pltpu.VMEM((LINE // 2, 2 * F, 2 * B), bf16),
            pltpu.VMEM((PLANE * B, R), f32),
            pltpu.VMEM((PLANE, B, R), bf16),
            pltpu.VMEM((PLANE, B, R), bf16),
            *sums, *sums, *sums,
            dma((LINE,)),
            dma((Z,)),
            dma((2,)),
            dma((PLANE,)),
            dma((1,)),
            dma((2,)),
            dma((2,)),
            dma((6,)),
            dma((6,)),
            dma((6,)),
        ],
        compiler_params=pltpu.CompilerParams(
            collective_id=0, has_side_effects=True, vmem_limit_bytes=VMEMLIM * 1024 * 1024
        ),
    )(features, targets)
    return pl.pallas_call(
        place,
        out_shape=(whole, whole, whole),
        in_specs=[vmem] * 3,
        out_specs=(vmem, vmem, vmem),
        compiler_params=pltpu.CompilerParams(vmem_limit_bytes=2 * 1024 * 1024),
    )(*results)


def solution(mesh):
    spec = P(None, ("col", "row"))
    return jax.shard_map(
        local, mesh=mesh, in_specs=(spec, spec), out_specs=(spec, spec, spec), check_vma=False
    )
```
